32 devices in a mesh: group: 2 (over x), latent: 16 (over z, y, core).
Axes of the slice: x: 2, y: 2, z: 4, core: 2. Of those that a mesh axis runs over, the one named last changes fastest.
Arguments:
- rows_in: bfloat16 [64, 3584], P(('group', 'latent')), parts along dimension 0, may hold values from -6 to 6
- active_ids: int32 [64, 128], P('group'), parts along dimension 0, may hold values from 0 to 2047, all different within a row
- encoder_weight: bfloat16 [7168, 2048], P('group', 'latent'), parts along dimension 0, may hold values from -0.09375 to 0.09375
- encoder_bias: float32 [4096], P(('group', 'latent')), parts along dimension 0, may hold values from -3 to 3
- threshold: float32 [4096], P(('group', 'latent')), parts along dimension 0, may hold values from 0.25 to 2
- decoder_weight: bfloat16 [4096, 3584], P(('group', 'latent')), parts along dimension 0, may hold values from -0.5 to 0.5
- decoder_bias: float32 [7168], P('group'), parts along dimension 0, may hold values from -3 to 3
Outputs:
- grad_encoder: bfloat16 [7168, 2048], P('group', 'latent'), parts along dimension 0
- grad_encoder_bias: float32 [4096], P(('group', 'latent')), parts along dimension 0
- grad_threshold: float32 [4096], P(('group', 'latent')), parts along dimension 0
- grad_decoder: bfloat16 [4096, 3584], P(('group', 'latent')), parts along dimension 0
- grad_decoder_bias: float32 [7168], P('group'), parts along dimension 0
The draws below stay inside these ranges and needn't reach their ends.
There are 2 independent parts, one for each index of `group`. The reference program is written for one: setup_inputs(seed, part) draws one part's arguments, and reference() takes and returns one part's arrays. A program takes and returns all parts, laid end to end along the dimension named above; each array names one. Nothing has to cross between parts.
Inputs may be any that keep to these rules, and one draw needn't show every extreme that they name: `active_ids`: each row names 128 different latents; every latent is named by some row.
All inputs are finite; a program needn't handle non-finite values.
Results may differ from the reference program's by a relative error of at most 0.0069.
Values may be sent and summed in bfloat16 or wider, within the bound.
No kernel may reach another device: no remote copies, remote signals or barrier semaphores. Data moves between devices by JAX's collectives and lax.ppermute only.
A program may use at most 64 MiB of HBM per device.

```python
import math
import jax
import jax.numpy as jnp
from jax import lax

D = 3584
ACTIVE = 128
ROWS = 32
LATENTS = 2048


def levels(own_key, shape, pieces, least, high):
    loudness, own = 1.0, jax.random.fold_in(own_key, 6)
    for position, blocks in pieces:
        heights = jnp.exp(jax.random.uniform(jax.random.fold_in(own, position), (blocks,), jnp.float32, least / len(pieces), high / len(pieces)))
        loudness = loudness * jnp.repeat(heights, shape[position] // blocks).reshape([-1 if axis == position else 1 for axis in range(len(shape))])
    return loudness


def distinct(rng, rows, amount, top, lift):
    sequence = jax.random.permutation(jax.random.fold_in(rng, 1), amount)
    favour = sequence
    for power in range(3):
        favour = favour * favour // amount
    favour = favour * lift // amount
    chance = jax.random.randint(jax.random.fold_in(rng, 2), (rows, amount), 0, 4096) + favour
    sure = jax.random.permutation(jax.random.fold_in(rng, 3), rows)[jnp.arange(amount) % rows]
    chance = jnp.where(jnp.arange(rows)[:, None] == sure[None, :], 1 << 14, chance)
    score = chance * amount + jnp.arange(amount)
    return lax.top_k(score.astype(jnp.int32), top)[1].astype(jnp.int32)


def normal_values(rng, extent, deviation, bound, shards=(), held_as=jnp.bfloat16):
    result = jax.random.normal(rng, extent, jnp.float32) * deviation
    if len(shards) > 0:
        result = levels(rng, extent, shards, -0.22, 0.18) * result
    return jnp.clip(result, min=-bound, max=bound).astype(held_as)


def setup_inputs(seed: int = 0, part: int = 0) -> dict:
    streams_of = jax.random.split(jax.random.key(seed), 8)
    part_keys = jax.random.split(jax.random.fold_in(streams_of[7], part), 8)
    rows_in = normal_values(part_keys[0], (ROWS, D), 1.0, 6.0, ((0, 16),))
    active_ids = distinct(part_keys[1], ROWS, LATENTS, ACTIVE, 1024)
    encoder_weight = normal_values(part_keys[2], (D, LATENTS), D ** -0.5, 0.09375, ((1, 16),))
    encoder_bias = normal_values(part_keys[3], (LATENTS,), 0.5, 3.0, ((0, 16),), jnp.float32)
    threshold = jnp.clip(jnp.exp(math.log(2.0) - 2.0794415 * jax.random.uniform(part_keys[4], (LATENTS,), jnp.float32) ** levels(part_keys[4], (LATENTS,), ((0, 16),), -0.2, 0.2)), 0.25, 2.0)
    decoder_weight = normal_values(part_keys[5], (LATENTS, D), ACTIVE ** -0.5, 0.5, ((0, 16),))
    decoder_bias = normal_values(part_keys[6], (D,), 0.5, 3.0, (), jnp.float32)
    return {"rows_in": rows_in, "active_ids": active_ids, "encoder_weight": encoder_weight, "encoder_bias": encoder_bias, "threshold": threshold, "decoder_weight": decoder_weight, "decoder_bias": decoder_bias}


EPSILON = 0.5
SPARSITY = 0.5

def reference(rows_in, active_ids, encoder_weight, encoder_bias, threshold, decoder_weight, decoder_bias):
    total_rows = rows_in.shape[0]
    centered = (rows_in.astype(jnp.float32) - decoder_bias).astype(jnp.bfloat16)
    preact = jnp.dot(centered, encoder_weight, preferred_element_type=jnp.float32) + encoder_bias
    row_index = jnp.broadcast_to(jnp.arange(total_rows, dtype=jnp.int32)[:, None], active_ids.shape)
    gating = jnp.zeros(preact.shape, jnp.float32).at[row_index, active_ids].set(1.0)
    latent_codes = (preact * gating).astype(jnp.bfloat16)
    rebuilt = jnp.dot(latent_codes, decoder_weight, preferred_element_type=jnp.float32) + decoder_bias
    errors = (rebuilt - rows_in.astype(jnp.float32)).astype(jnp.bfloat16)
    code_grad = jnp.dot(errors, decoder_weight.T, preferred_element_type=jnp.float32)
    distance = (preact - threshold) / EPSILON
    kernel = jnp.exp(-0.5 * distance * distance) / (EPSILON * math.sqrt(2.0 * math.pi))
    grad_threshold = lax.optimization_barrier(jnp.sum(-threshold * code_grad * kernel - SPARSITY * kernel, axis=0))
    preact_grad = code_grad * gating
    grad_encoder_bias = lax.optimization_barrier(jnp.sum(preact_grad, axis=0))
    preact_low = preact_grad.astype(jnp.bfloat16)
    grad_encoder = jnp.dot(centered.T, preact_low, preferred_element_type=jnp.float32).astype(jnp.bfloat16)
    grad_decoder = jnp.dot(latent_codes.T, errors, preferred_element_type=jnp.float32).astype(jnp.bfloat16)
    encoder_part = jnp.dot(encoder_weight, grad_encoder_bias, preferred_element_type=jnp.float32, precision=lax.Precision.HIGHEST)
    grad_decoder_bias = lax.optimization_barrier(jnp.sum(errors, axis=0, dtype=jnp.float32)) - encoder_part
    return (grad_encoder, grad_encoder_bias, grad_threshold, grad_decoder, grad_decoder_bias)
```

```python
import math

import jax
import jax.numpy as jnp
from jax import lax
from jax.sharding import PartitionSpec as P

EPSILON = 0.5
SPARSITY = 0.5
F32 = jnp.float32
BF16 = jnp.bfloat16


def opened(ids, offset, width):
    latent = offset + lax.broadcasted_iota(jnp.int32, (1, 1, width), 2)
    return jnp.any(ids[:, :, None] == latent, axis=1)


def on_device(
    count, rows_in, active_ids, encoder_weight, encoder_bias, threshold, decoder_weight, decoder_bias
):
    width = encoder_weight.shape[1]
    me = lax.axis_index("latent")
    core = me & 1

    def swap(array, bit):
        return lax.ppermute(array, "latent", [(i, i ^ bit) for i in range(count)])

    hops = []
    bit = 2
    while bit < count:
        hops.append(bit)
        bit *= 2

    encoder_other = swap(encoder_weight, 1)
    decoder_other = swap(decoder_weight, 1)
    bias_other = swap(encoder_bias, 1)

    per_device, depth = rows_in.shape
    block = rows_in[None]
    for bit in hops:
        other = swap(block, bit)
        low = jnp.concatenate([block, other], axis=0)
        high = jnp.concatenate([other, block], axis=0)
        block = jnp.where((me & bit) == 0, low, high)
    half_rows = block.shape[0] * per_device
    rows = block.reshape(half_rows, depth)

    ids = active_ids.reshape(half_rows // per_device, 2, per_device, active_ids.shape[1])
    ids_mine = lax.dynamic_index_in_dim(ids, core, 1, keepdims=False).reshape(half_rows, -1)
    ids_other = lax.dynamic_index_in_dim(ids, 1 - core, 1, keepdims=False).reshape(half_rows, -1)

    def center(part):
        return (part.astype(F32) - decoder_bias).astype(BF16)

    def dot(a, b):
        return jnp.dot(a, b, preferred_element_type=F32)

    def dot_last(a, b):
        return lax.dot_general(a, b, (((1,), (1,)), ((), ())), preferred_element_type=F32)

    def dot_rows(a, b):
        return lax.dot_general(a, b, (((0,), (0,)), ((), ())), preferred_element_type=F32)

    centered = center(rows)
    gate_mine = opened(ids_mine, me * width, width)
    gate_other = opened(ids_mine, (me ^ 1) * width, width)
    preact_mine = dot(centered, encoder_weight) + encoder_bias
    preact_other = dot(centered, encoder_other) + bias_other
    codes_mine = jnp.where(gate_mine, preact_mine, 0.0).astype(BF16)
    codes_other = jnp.where(gate_other, preact_other, 0.0).astype(BF16)
    total = dot(codes_mine, decoder_weight) + dot(codes_other, decoder_other)
    for bit in hops:
        low = lax.optimization_barrier(total.astype(BF16))
        total = low.astype(F32) + swap(low, bit).astype(F32)
    errors = lax.optimization_barrier((total + decoder_bias - rows.astype(F32)).astype(BF16))

    grad_mine = jnp.sum(jnp.where(gate_mine, dot_last(errors, decoder_weight), 0.0), axis=0)
    grad_other = jnp.sum(jnp.where(gate_other, dot_last(errors, decoder_other), 0.0), axis=0)

    def product(weight, vector):
        upper = vector.astype(BF16)
        lower = (vector - upper.astype(F32)).astype(BF16)
        both = jnp.stack([upper, lower])
        return dot_last(both, weight)

    part = product(encoder_weight, grad_mine) + product(encoder_other, grad_other)
    part = part[0] + part[1]
    for bit in hops:
        part = part + swap(part, bit)
    part = jnp.sum(errors, axis=0, dtype=F32) - part
    grad_decoder_bias = part + swap(part, 1)

    rows_other = swap(rows, 1)
    errors_other = swap(errors, 1)
    centered_other = center(rows_other)
    gate_rest = opened(ids_other, me * width, width)
    preact_rest = dot(centered_other, encoder_weight) + encoder_bias
    preact = jnp.concatenate([preact_mine, preact_rest])
    gate = jnp.concatenate([gate_mine, gate_rest])
    every_error = jnp.concatenate([errors, errors_other])
    every_centered = jnp.concatenate([centered, centered_other])
    codes = jnp.where(gate, preact, 0.0).astype(BF16)
    code_grad = dot_last(every_error, decoder_weight)
    distance = (preact - threshold) / EPSILON
    kernel = jnp.exp(-0.5 * distance * distance) / (EPSILON * math.sqrt(2.0 * math.pi))
    grad_threshold = jnp.sum(-threshold * code_grad * kernel - SPARSITY * kernel, axis=0)
    preact_grad = jnp.where(gate, code_grad, 0.0)
    grad_encoder_bias = jnp.sum(preact_grad, axis=0)
    grad_encoder = dot_rows(every_centered, preact_grad.astype(BF16)).astype(BF16)
    grad_decoder = dot_rows(codes, every_error).astype(BF16)
    return (grad_encoder, grad_encoder_bias, grad_threshold, grad_decoder, grad_decoder_bias)


def solution(mesh):
    count = mesh.shape["latent"]

    def body(*args):
        return on_device(count, *args)

    placed = (
        P(("group", "latent"), None),
        P("group", None),
        P("group", "latent"),
        P(("group", "latent")),
        P(("group", "latent")),
        P(("group", "latent"), None),
        P("group"),
    )
    return jax.shard_map(
        body,
        mesh=mesh,
        in_specs=placed,
        out_specs=(
            P("group", "latent"),
            P(("group", "latent")),
            P(("group", "latent")),
            P(("group", "latent"), None),
            P("group"),
        ),
        check_vma=False,
    )
```

```python
import math

import jax
import jax.numpy as jnp
from jax import lax
from jax.sharding import PartitionSpec as P

EPSILON = 0.5
SPARSITY = 0.5
F32 = jnp.float32
BF16 = jnp.bfloat16


def opened(ids, offset, width):
    latent = offset + lax.broadcasted_iota(jnp.int32, (1, 1, width), 2)
    return jnp.any(ids[:, :, None] == latent, axis=1)


def on_device(
    count, rows_in, active_ids, encoder_weight, encoder_bias, threshold, decoder_weight, decoder_bias
):
    width = encoder_weight.shape[1]
    me = lax.axis_index("latent")
    core = me & 1

    def swap(array, bit):
        return lax.ppermute(array, "latent", [(i, i ^ bit) for i in range(count)])

    hops = []
    bit = 2
    while bit < count:
        hops.append(bit)
        bit *= 2

    encoder_other = swap(encoder_weight, 1)
    decoder_other = swap(decoder_weight, 1)
    bias_other = swap(encoder_bias, 1)

    per_device, depth = rows_in.shape
    block = rows_in[None]
    for bit in hops:
        other = swap(block, bit)
        low = jnp.concatenate([block, other], axis=0)
        high = jnp.concatenate([other, block], axis=0)
        block = jnp.where((me & bit) == 0, low, high)
    half_rows = block.shape[0] * per_device
    rows = block.reshape(half_rows, depth)

    ids = active_ids.reshape(half_rows // per_device, 2, per_device, active_ids.shape[1])
    ids_mine = lax.dynamic_index_in_dim(ids, core, 1, keepdims=False).reshape(half_rows, -1)
    ids_other = lax.dynamic_index_in_dim(ids, 1 - core, 1, keepdims=False).reshape(half_rows, -1)

    def center(part):
        return (part.astype(F32) - decoder_bias).astype(BF16)

    def dot(a, b):
        return jnp.dot(a, b, preferred_element_type=F32)

    def dot_last(a, b):
        return lax.dot_general(a, b, (((1,), (1,)), ((), ())), preferred_element_type=F32)

    def dot_rows(a, b):
        return lax.dot_general(a, b, (((0,), (0,)), ((), ())), preferred_element_type=F32)

    centered = center(rows)
    gate_mine = opened(ids_mine, me * width, width)
    gate_other = opened(ids_mine, (me ^ 1) * width, width)
    preact_mine = dot(centered, encoder_weight) + encoder_bias
    preact_other = dot(centered, encoder_other) + bias_other
    codes_mine = jnp.where(gate_mine, preact_mine, 0.0).astype(BF16)
    codes_other = jnp.where(gate_other, preact_other, 0.0).astype(BF16)
    total = dot(codes_mine, decoder_weight) + dot(codes_other, decoder_other)
    rows_other = swap(rows, 1)
    centered_other = center(rows_other)
    gate_rest = opened(ids_other, me * width, width)
    preact_rest = dot(centered_other, encoder_weight) + encoder_bias
    preact = jnp.concatenate([preact_mine, preact_rest])
    gate = jnp.concatenate([gate_mine, gate_rest])
    every_centered = jnp.concatenate([centered, centered_other])
    codes = jnp.where(gate, preact, 0.0).astype(BF16)

    for bit in hops:
        low = lax.optimization_barrier(total.astype(BF16))
        total = low.astype(F32) + swap(low, bit).astype(F32)
    errors = lax.optimization_barrier((total + decoder_bias - rows.astype(F32)).astype(BF16))

    grad_mine = jnp.sum(jnp.where(gate_mine, dot_last(errors, decoder_weight), 0.0), axis=0)
    grad_other = jnp.sum(jnp.where(gate_other, dot_last(errors, decoder_other), 0.0), axis=0)

    def product(weight, vector):
        upper = vector.astype(BF16)
        lower = (vector - upper.astype(F32)).astype(BF16)
        both = jnp.stack([upper, lower])
        return dot_last(both, weight)

    part = product(encoder_weight, grad_mine) + product(encoder_other, grad_other)
    part = part[0] + part[1]
    errors_other = swap(errors, 1)

    every_error = jnp.concatenate([errors, errors_other])

    def small_outputs():
        code_grad = dot_last(every_error, decoder_weight)
        distance = (preact - threshold) / EPSILON
        kernel = jnp.exp(-0.5 * distance * distance) / (EPSILON * math.sqrt(2.0 * math.pi))
        grad_threshold = jnp.sum(-threshold * code_grad * kernel - SPARSITY * kernel, axis=0)
        preact_grad = jnp.where(gate, code_grad, 0.0)
        return grad_threshold, jnp.sum(preact_grad, axis=0), preact_grad.astype(BF16)

    def decoder_output():
        return dot_rows(codes, every_error).astype(BF16)

    def encoder_output():
        return dot_rows(every_centered, small[2]).astype(BF16)

    part = part + swap(part, hops[0])
    small, part = lax.optimization_barrier((small_outputs(), part))
    part = part + swap(part, hops[1])
    grad_decoder, part = lax.optimization_barrier((decoder_output(), part))
    part = part + swap(part, hops[2])
    grad_encoder, part = lax.optimization_barrier((encoder_output(), part))
    for bit in hops[3:]:
        part = part + swap(part, bit)
    part = jnp.sum(errors, axis=0, dtype=F32) - part
    grad_decoder_bias = part + swap(part, 1)
    grad_threshold, grad_encoder_bias, _ = small
    return (grad_encoder, grad_encoder_bias, grad_threshold, grad_decoder, grad_decoder_bias)


def solution(mesh):
    count = mesh.shape["latent"]

    def body(*args):
        return on_device(count, *args)

    placed = (
        P(("group", "latent"), None),
        P("group", None),
        P("group", "latent"),
        P(("group", "latent")),
        P(("group", "latent")),
        P(("group", "latent"), None),
        P("group"),
    )
    return jax.shard_map(
        body,
        mesh=mesh,
        in_specs=placed,
        out_specs=(
            P("group", "latent"),
            P(("group", "latent")),
            P(("group", "latent")),
            P(("group", "latent"), None),
            P("group"),
        ),
        check_vma=False,
    )
```

```python
import math

import jax
import jax.numpy as jnp
from jax import lax
from jax.experimental import pallas as pl
from jax.experimental.pallas import tpu as pltpu
from jax.sharding import PartitionSpec as P

EPSILON = 0.5
SPARSITY = 0.5
F32 = jnp.float32
BF16 = jnp.bfloat16
LIMIT = 12 * 1024 * 1024


def opened(ids, offset, width):
    latent = offset + lax.broadcasted_iota(jnp.int32, (1, 1, width), 2)
    return jnp.any(ids[:, :, None] == latent, axis=1)


def dot(a, b):
    return jnp.dot(a, b, preferred_element_type=F32)


def dot_last(a, b):
    return lax.dot_general(a, b, (((1,), (1,)), ((), ())), preferred_element_type=F32)


def dot_rows(a, b):
    return lax.dot_general(a, b, (((0,), (0,)), ((), ())), preferred_element_type=F32)


def forward_kernel(
    block, received, first, decoder_bias, gates, encoder, encoder_other, bias, bias_other, decoder,
    decoder_other, rows, centered, preact, partial
):
    width = encoder.shape[1]
    lead = first[0:1, 0:1] > 0.0
    here, there = block[...].astype(F32), received[...].astype(F32)
    every = jnp.concatenate([jnp.where(lead, here, there), jnp.where(lead, there, here)], axis=0)
    rows[...] = every.astype(BF16)
    shifted = (every - decoder_bias[...]).astype(BF16)
    centered[...] = shifted
    mine = dot(shifted, encoder[...]) + bias[...]
    other = dot(shifted, encoder_other[...]) + bias_other[...]
    preact[...] = mine
    codes = (mine * gates[:, :width]).astype(BF16)
    codes_other = (other * gates[:, width:]).astype(BF16)
    partial[...] = (dot(codes, decoder[...]) + dot(codes_other, decoder_other[...])).astype(BF16)


def backward_kernel(
    low, received, rows, decoder_bias, gates, encoder, encoder_other, decoder, decoder_other,
    errors, error_sum, part
):
    width = encoder.shape[1]
    total = low[...].astype(F32) + received[...].astype(F32)
    found = (total + decoder_bias[...] - rows[...].astype(F32)).astype(BF16)
    errors[...] = found
    error_sum[...] = jnp.sum(found.astype(F32), axis=0, keepdims=True)

    def product(gate, decoder_block, encoder_block):
        grad = jnp.sum(dot_last(found, decoder_block[...]) * gate, axis=0, keepdims=True)
        upper = grad.astype(BF16).astype(F32)
        row = lax.broadcasted_iota(jnp.int32, (8, width), 0)
        both = jnp.where(row == 0, upper, jnp.where(row == 1, grad - upper, 0.0))
        return dot_last(both.astype(BF16), encoder_block[...])

    both = product(gates[:, :width], decoder, encoder)
    both += product(gates[:, width:], decoder_other, encoder_other)
    part[...] = jnp.sum(both, axis=0, keepdims=True)


def stage_kernel(*refs):
    half = (len(refs) - 1) // 2
    copies = [
        pltpu.make_async_copy(
            source, target if len(source.shape) > 1 else target.at[0], refs[-1].at[i]
        )
        for i, (source, target) in enumerate(zip(refs[:half], refs[half:-1]))
    ]
    for copy in copies:
        copy.start()
    for copy in copies:
        copy.wait()


def stage(*arrays):
    shapes = [array.shape if array.ndim > 1 else (1,) + array.shape for array in arrays]
    return pl.pallas_call(
        stage_kernel,
        in_specs=[pl.BlockSpec(memory_space=pltpu.HBM)] * len(arrays),
        out_specs=[pl.BlockSpec(memory_space=pltpu.VMEM)] * len(arrays),
        out_shape=[pltpu.VMEM(shape, array.dtype) for shape, array in zip(shapes, arrays)],
        scratch_shapes=[pltpu.SemaphoreType.DMA((len(arrays),))],
        compiler_params=pltpu.CompilerParams(vmem_limit_bytes=LIMIT),
    )(*[pltpu.with_memory_space_constraint(array, pltpu.HBM) for array in arrays])


def near(kernel, arrays, outs):
    whole = pl.BlockSpec(memory_space=pltpu.VMEM)
    return pl.pallas_call(
        kernel,
        in_specs=[whole] * len(arrays),
        out_specs=[whole] * len(outs),
        out_shape=[pltpu.VMEM(shape, dtype) for shape, dtype in outs],
        compiler_params=pltpu.CompilerParams(vmem_limit_bytes=LIMIT),
    )(*[pltpu.with_memory_space_constraint(array, pltpu.VMEM) for array in arrays])


def on_device(
    count, rows_in, active_ids, encoder_weight, encoder_bias, threshold, decoder_weight, decoder_bias
):
    width = encoder_weight.shape[1]
    me = lax.axis_index("latent")
    core = me & 1

    def swap(array, bit):
        return lax.ppermute(array, "latent", [(i, i ^ bit) for i in range(count)])

    hops = []
    bit = 2
    while bit < count:
        hops.append(bit)
        bit *= 2

    encoder_other = swap(encoder_weight, 1)
    decoder_other = swap(decoder_weight, 1)
    bias_other = swap(encoder_bias[None], 1)

    per_device, depth = rows_in.shape
    block, bias_row = stage(rows_in, decoder_bias)
    for bit in hops[:-1]:
        other = swap(rows_in if bit == hops[0] else block, bit)
        low = jnp.concatenate([block, other], axis=0)
        high = jnp.concatenate([other, block], axis=0)
        block = jnp.where((me & bit) == 0, low, high)
    weights = (encoder_weight, decoder_weight, encoder_bias)
    block, weights = lax.optimization_barrier((block, weights))
    received = swap(block, hops[-1])
    encoder_near, decoder_near, encoder_row = stage(*weights)
    first = jnp.full((1, width), jnp.where((me & hops[-1]) == 0, 1.0, 0.0), F32)
    half_rows = 2 * block.shape[0]

    ids = active_ids.reshape(half_rows // per_device, 2, per_device, active_ids.shape[1])
    ids_mine = lax.dynamic_index_in_dim(ids, core, 1, keepdims=False).reshape(half_rows, -1)
    ids_other = lax.dynamic_index_in_dim(ids, 1 - core, 1, keepdims=False).reshape(half_rows, -1)

    def center(part):
        return (part.astype(F32) - bias_row).astype(BF16)

    gate_mine = opened(ids_mine, me * width, width)
    gates = jnp.concatenate([gate_mine, opened(ids_mine, (me ^ 1) * width, width)], axis=1)
    gates = gates.astype(F32)
    rows, centered, preact_mine, partial = near(
        forward_kernel,
        (block, received, first, bias_row, gates, encoder_near, encoder_other, encoder_row, bias_other,
         decoder_near, decoder_other),
        (
            ((half_rows, depth), BF16),
            ((half_rows, depth), BF16),
            ((half_rows, width), F32),
            ((half_rows, depth), BF16),
        ),
    )

    rows_other = swap(rows, 1)
    centered_other = center(rows_other)
    gate_rest = opened(ids_other, me * width, width)
    preact_rest = dot(centered_other, encoder_near) + encoder_row
    preact = jnp.concatenate([preact_mine, preact_rest])
    gate = jnp.concatenate([gate_mine, gate_rest])
    every_centered = jnp.concatenate([centered, centered_other])
    codes = jnp.where(gate, preact, 0.0).astype(BF16)

    for bit in hops[:-1]:
        partial = partial + swap(partial, bit)
        partial = lax.optimization_barrier(partial)
    partial, weights = lax.optimization_barrier((partial, (encoder_weight, decoder_weight)))
    received = swap(partial, hops[-1])
    encoder_near, decoder_near = stage(*weights)
    errors, error_sum, part = near(
        backward_kernel,
        (partial, received, rows, bias_row, gates, encoder_near, encoder_other, decoder_near,
         decoder_other),
        (((half_rows, depth), BF16), ((1, depth), F32), ((1, depth), F32)),
    )
    errors_other = swap(errors, 1)

    every_error = jnp.concatenate([errors, errors_other])

    def small_outputs():
        code_grad = dot_last(every_error, decoder_near)
        distance = (preact - threshold) / EPSILON
        kernel = jnp.exp(-0.5 * distance * distance) / (EPSILON * math.sqrt(2.0 * math.pi))
        grad_threshold = jnp.sum(-threshold * code_grad * kernel - SPARSITY * kernel, axis=0)
        preact_grad = jnp.where(gate, code_grad, 0.0)
        return grad_threshold, jnp.sum(preact_grad, axis=0), preact_grad.astype(BF16)

    def decoder_output():
        return dot_rows(codes, every_error).astype(BF16)

    def encoder_output():
        return dot_rows(every_centered, small[2]).astype(BF16)

    part = part + swap(part, hops[0])
    small, part = lax.optimization_barrier((small_outputs(), part))
    part = part + swap(part, hops[1])
    grad_decoder, part = lax.optimization_barrier((decoder_output(), part))
    part = part + swap(part, hops[2])
    grad_encoder, part = lax.optimization_barrier((encoder_output(), part))
    for bit in hops[3:]:
        part = part + swap(part, bit)
    part = error_sum - part
    grad_decoder_bias = (part + swap(part, 1)).reshape(depth)
    grad_threshold, grad_encoder_bias, _ = small
    return (grad_encoder, grad_encoder_bias, grad_threshold, grad_decoder, grad_decoder_bias)


def solution(mesh):
    count = mesh.shape["latent"]

    def body(*args):
        return on_device(count, *args)

    placed = (
        P(("group", "latent"), None),
        P("group", None),
        P("group", "latent"),
        P(("group", "latent")),
        P(("group", "latent")),
        P(("group", "latent"), None),
        P("group"),
    )
    return jax.shard_map(
        body,
        mesh=mesh,
        in_specs=placed,
        out_specs=(
            P("group", "latent"),
            P(("group", "latent")),
            P(("group", "latent")),
            P(("group", "latent"), None),
            P("group"),
        ),
        check_vma=False,
    )
```

```python
import math

import jax
import jax.numpy as jnp
from jax import lax
from jax.experimental import pallas as pl
from jax.experimental.pallas import tpu as pltpu
from jax.sharding import PartitionSpec as P

EPSILON = 0.5
SPARSITY = 0.5
F32 = jnp.float32
BF16 = jnp.bfloat16
LIMIT = 12 * 1024 * 1024


def opened(ids, offset, width):
    latent = offset + lax.broadcasted_iota(jnp.int32, (1, 1, width), 2)
    return jnp.any(ids[:, :, None] == latent, axis=1)


def dot(a, b):
    return jnp.dot(a, b, preferred_element_type=F32)


def dot_last(a, b):
    return lax.dot_general(a, b, (((1,), (1,)), ((), ())), preferred_element_type=F32)


def dot_rows(a, b):
    return lax.dot_general(a, b, (((0,), (0,)), ((), ())), preferred_element_type=F32)


def forward_kernel(
    rows, decoder_bias, gates, encoder, encoder_other, bias, bias_other, decoder, decoder_other,
    preact, partial
):
    width = encoder.shape[1]
    centered = (rows[...].astype(F32) - decoder_bias[...]).astype(BF16)
    mine = dot(centered, encoder[...]) + bias[...]
    other = dot(centered, encoder_other[...]) + bias_other[...]
    preact[...] = mine
    codes = (mine * gates[:, :width]).astype(BF16)
    codes_other = (other * gates[:, width:]).astype(BF16)
    partial[...] = (dot(codes, decoder[...]) + dot(codes_other, decoder_other[...])).astype(BF16)


def backward_kernel(
    low, low_received, rows, gates, high, high_received, rows_far, gates_far, decoder_bias,
    encoder, encoder_other, decoder, decoder_other, errors, sums
):
    width = encoder.shape[1]

    def error(total, received, block):
        total = total[...].astype(F32) + received[...].astype(F32)
        return (total + decoder_bias[...] - block[...].astype(F32)).astype(BF16).astype(F32)

    near_part = error(low, low_received, rows)
    far_part = error(high, high_received, rows_far)
    sums[0:1, :] = jnp.sum(near_part, axis=0, keepdims=True) + jnp.sum(
        far_part, axis=0, keepdims=True
    )
    found = jnp.concatenate([near_part, far_part], axis=0).astype(BF16)
    errors[...] = found
    gate = jnp.concatenate([gates[...], gates_far[...]], axis=0)

    def product(gate, decoder_block, encoder_block):
        grad = jnp.sum(dot_last(found, decoder_block[...]) * gate, axis=0, keepdims=True)
        upper = grad.astype(BF16).astype(F32)
        row = lax.broadcasted_iota(jnp.int32, (8, width), 0)
        both = jnp.where(row == 0, upper, jnp.where(row == 1, grad - upper, 0.0))
        return dot_last(both.astype(BF16), encoder_block[...])

    both = product(gate[:, :width], decoder, encoder)
    both += product(gate[:, width:], decoder_other, encoder_other)
    sums[1:2, :] = jnp.sum(both, axis=0, keepdims=True)


def size(array):
    return array.size * array.dtype.itemsize


def cost(moved):
    return pl.CostEstimate(flops=0, bytes_accessed=moved, transcendentals=0)


def stage_kernel(*refs):
    half = (len(refs) - 1) // 2
    copies = [
        pltpu.make_async_copy(
            source, target if len(source.shape) > 1 else target.at[0], refs[-1].at[i]
        )
        for i, (source, target) in enumerate(zip(refs[:half], refs[half:-1]))
    ]
    for copy in copies:
        copy.start()
    for copy in copies:
        copy.wait()


def stage(*arrays):
    shapes = [array.shape if array.ndim > 1 else (1,) + array.shape for array in arrays]
    return pl.pallas_call(
        stage_kernel,
        in_specs=[pl.BlockSpec(memory_space=pltpu.HBM)] * len(arrays),
        out_specs=[pl.BlockSpec(memory_space=pltpu.VMEM)] * len(arrays),
        out_shape=[pltpu.VMEM(shape, array.dtype) for shape, array in zip(shapes, arrays)],
        scratch_shapes=[pltpu.SemaphoreType.DMA((len(arrays),))],
        cost_estimate=cost(2 * sum(size(array) for array in arrays)),
        compiler_params=pltpu.CompilerParams(vmem_limit_bytes=LIMIT),
    )(*[pltpu.with_memory_space_constraint(array, pltpu.HBM) for array in arrays])


def near(kernel, arrays, outs):
    whole = pl.BlockSpec(memory_space=pltpu.VMEM)
    return pl.pallas_call(
        kernel,
        in_specs=[whole] * len(arrays),
        out_specs=[whole] * len(outs),
        out_shape=[pltpu.VMEM(shape, dtype) for shape, dtype in outs],
        cost_estimate=cost(sum(size(array) for array in arrays)),
        compiler_params=pltpu.CompilerParams(vmem_limit_bytes=LIMIT),
    )(*[pltpu.with_memory_space_constraint(array, pltpu.VMEM) for array in arrays])


def after(first, array):
    return lax.optimization_barrier((first, array))[1]


def on_device(
    count, rows_in, active_ids, encoder_weight, encoder_bias, threshold, decoder_weight, decoder_bias
):
    width = encoder_weight.shape[1]
    me = lax.axis_index("latent")
    core = me & 1

    def swap(array, bit):
        return lax.ppermute(array, "latent", [(i, i ^ bit) for i in range(count)])

    hops = []
    bit = 2
    while bit < count:
        hops.append(bit)
        bit *= 2

    encoder_other = swap(encoder_weight, 1)
    decoder_other = swap(decoder_weight, 1)
    bias_other = swap(encoder_bias[None], 1)

    per_device, depth = rows_in.shape
    block, bias_row = stage(rows_in, decoder_bias)
    for bit in hops[:-1]:
        if bit == hops[-2]:
            weights = (encoder_weight, decoder_weight, encoder_bias)
            block, weights = lax.optimization_barrier((block, weights))
        other = swap(rows_in if bit == hops[0] else block, bit)
        low = jnp.concatenate([block, other], axis=0)
        high = jnp.concatenate([other, block], axis=0)
        block = jnp.where((me & bit) == 0, low, high)
    encoder_near, decoder_near, encoder_row = stage(*weights)
    block, encoder_near, decoder_near, encoder_row = lax.optimization_barrier(
        (block, encoder_near, decoder_near, encoder_row)
    )
    rows = block
    rows_far = swap(block, hops[-1])
    half_rows = rows.shape[0]

    ids = active_ids.reshape(2, half_rows // per_device, 2, per_device, active_ids.shape[1])
    side = jnp.where((me & hops[-1]) == 0, 0, 1)

    def listed(half, part):
        one = lax.dynamic_index_in_dim(ids, half, 0, keepdims=False)
        one = lax.dynamic_index_in_dim(one, part, 1, keepdims=False)
        return one.reshape(half_rows, -1)

    def center(part):
        return (part.astype(F32) - bias_row).astype(BF16)

    lists = jnp.concatenate([listed(side, core), listed(1 - side, core)])
    lists_other = jnp.concatenate([listed(side, 1 - core), listed(1 - side, 1 - core)])
    gate_mine = opened(lists, me * width, width)
    gates = jnp.concatenate([gate_mine, opened(lists, (me ^ 1) * width, width)], axis=1)
    gates = gates.astype(F32)
    gates, gates_far = gates[:half_rows], gates[half_rows:]

    def forward(part, gate):
        return near(
            forward_kernel,
            (part, bias_row, gate, encoder_near, encoder_other, encoder_row, bias_other,
             decoder_near, decoder_other),
            (((half_rows, width), F32), ((half_rows, depth), BF16)),
        )

    preact_near, low = forward(rows, gates)
    preact_far, high = forward(after(low, rows_far), gates_far)
    every_row = jnp.concatenate([rows, after(high, rows_far)])
    for bit in hops[:-1]:
        low, high_received = lax.optimization_barrier(low + swap(low, bit)), swap(high, bit)
        high = lax.optimization_barrier(high + after(low, high_received))
    high_received = swap(low, hops[-1])
    high, weights = lax.optimization_barrier((high, (encoder_weight, decoder_weight)))
    low_received = swap(high, hops[-1])
    encoder_near, decoder_near = stage(*weights)

    rows_other = swap(every_row, 1)
    centered_other = center(rows_other)
    gate_rest = opened(lists_other, me * width, width)
    preact_rest = dot(centered_other, encoder_weight) + encoder_bias
    preact = jnp.concatenate([preact_near, preact_far, preact_rest])
    gate = jnp.concatenate([gate_mine, gate_rest])
    every_centered = jnp.concatenate([center(every_row), centered_other])
    codes = jnp.where(gate, preact, 0.0).astype(BF16)

    errors, sums = near(
        backward_kernel,
        (low, low_received, rows, gates, high, high_received, rows_far, gates_far, bias_row,
         encoder_near, encoder_other, decoder_near, decoder_other),
        (((2 * half_rows, depth), BF16), ((2, depth), F32)),
    )
    errors_other = swap(errors, 1)
    sums = sums + swap(sums, 1)
    errors_other, sums = lax.optimization_barrier((errors_other, sums))
    part = sums[1:]

    every_error = jnp.concatenate([errors, errors_other])

    def small_outputs():
        code_grad = dot_last(every_error, decoder_near)
        distance = (preact - threshold) / EPSILON
        kernel = jnp.exp(-0.5 * distance * distance) / (EPSILON * math.sqrt(2.0 * math.pi))
        grad_threshold = jnp.sum(-threshold * code_grad * kernel - SPARSITY * kernel, axis=0)
        preact_grad = jnp.where(gate, code_grad, 0.0)
        return grad_threshold, jnp.sum(preact_grad, axis=0), preact_grad.astype(BF16)

    def decoder_output():
        return dot_rows(codes, every_error).astype(BF16)

    def encoder_output():
        return dot_rows(every_centered, small[2]).astype(BF16)

    part = part + swap(part, hops[0])
    small, part = lax.optimization_barrier((small_outputs(), part))
    part = part + swap(part, hops[1])
    grad_decoder, part = lax.optimization_barrier((decoder_output(), part))
    for bit in hops[2:]:
        part = part + swap(part, bit)
    grad_decoder_bias = (sums[:1] - part).reshape(depth)
    grad_encoder = encoder_output()
    grad_threshold, grad_encoder_bias, _ = small
    return (grad_encoder, grad_encoder_bias, grad_threshold, grad_decoder, grad_decoder_bias)


def solution(mesh):
    count = mesh.shape["latent"]

    def body(*args):
        return on_device(count, *args)

    placed = (
        P(("group", "latent"), None),
        P("group", None),
        P("group", "latent"),
        P(("group", "latent")),
        P(("group", "latent")),
        P(("group", "latent"), None),
        P("group"),
    )
    return jax.shard_map(
        body,
        mesh=mesh,
        in_specs=placed,
        out_specs=(
            P("group", "latent"),
            P(("group", "latent")),
            P(("group", "latent")),
            P(("group", "latent"), None),
            P("group"),
        ),
        check_vma=False,
    )
```

```python
import math

import jax
import jax.numpy as jnp
from jax import lax
from jax.experimental import pallas as pl
from jax.experimental.pallas import tpu as pltpu
from jax.sharding import PartitionSpec as P

EPSILON = 0.5
SPARSITY = 0.5
F32 = jnp.float32
BF16 = jnp.bfloat16
LIMIT = 12 * 1024 * 1024


def opened(ids, offset, width):
    latent = offset + lax.broadcasted_iota(jnp.int32, (1, 1, width), 2)
    return jnp.any(ids[:, :, None] == latent, axis=1)


def dot(a, b):
    return jnp.dot(a, b, preferred_element_type=F32)


def dot_last(a, b):
    return lax.dot_general(a, b, (((1,), (1,)), ((), ())), preferred_element_type=F32)


def dot_rows(a, b):
    return lax.dot_general(a, b, (((0,), (0,)), ((), ())), preferred_element_type=F32)


def forward_kernel(
    rows, decoder_bias, gates, encoder, encoder_other, bias, bias_other, decoder, decoder_other,
    preact, partial
):
    width = encoder.shape[1]
    centered = (rows[...].astype(F32) - decoder_bias[...]).astype(BF16)
    mine = dot(centered, encoder[...]) + bias[...]
    other = dot(centered, encoder_other[...]) + bias_other[...]
    preact[...] = mine
    codes = (mine * gates[:, :width]).astype(BF16)
    codes_other = (other * gates[:, width:]).astype(BF16)
    partial[...] = (dot(codes, decoder[...]) + dot(codes_other, decoder_other[...])).astype(BF16)


def backward_kernel(
    low, low_received, rows, gates, high, high_received, rows_far, gates_far, decoder_bias,
    encoder_turned, decoder_turned, errors, part
):
    def error(total, received, block):
        total = total[...].astype(F32) + received[...].astype(F32)
        return total + decoder_bias[...] - block[...].astype(F32)

    found = jnp.concatenate(
        [error(low, low_received, rows), error(high, high_received, rows_far)], axis=0
    ).astype(BF16)
    errors[...] = found
    gate = jnp.concatenate([gates[...], gates_far[...]], axis=0)
    width = gate.shape[1] // 2
    mine, other = dot(found, decoder_turned[:, :width]), dot(found, decoder_turned[:, width:])
    code_grad = jnp.concatenate([mine, other], axis=1)
    grad = jnp.sum(code_grad * gate, axis=0, keepdims=True)
    upper = grad.astype(BF16).astype(F32)
    row = lax.broadcasted_iota(jnp.int32, (8, grad.shape[1]), 0)
    both = jnp.where(row == 0, upper, jnp.where(row == 1, grad - upper, 0.0))
    spread = dot(both.astype(BF16), encoder_turned[...])
    part[...] = spread[0:1, :] + spread[1:2, :]


def sum_kernel(errors, errors_other, total):
    half = errors.shape[0] // 2

    def summed(ref):
        block = ref[...].astype(F32)
        first = jnp.sum(block[:half], axis=0, keepdims=True)
        return first + jnp.sum(block[half:], axis=0, keepdims=True)

    total[...] = summed(errors) + summed(errors_other)


def turn_kernel(
    encoder_far, decoder_far, encoder_other, decoder_other, encoder_turned, decoder_turned,
    encoder, decoder, ready
):
    first = pltpu.make_async_copy(decoder_far, decoder, ready.at[0])
    second = pltpu.make_async_copy(encoder_far, encoder, ready.at[1])
    first.start()
    second.start()
    width = encoder_other.shape[1]
    decoder_turned[:, width:] = decoder_other[...].T
    encoder_turned[width:, :] = encoder_other[...].T
    first.wait()
    decoder_turned[:, :width] = decoder[...].T
    second.wait()
    encoder_turned[:width, :] = encoder[...].T


def turn(encoder, decoder, encoder_other, decoder_other):
    depth, width = encoder.shape
    far = pl.BlockSpec(memory_space=pltpu.HBM)
    whole = pl.BlockSpec(memory_space=pltpu.VMEM)
    return pl.pallas_call(
        turn_kernel,
        in_specs=[far, far, whole, whole],
        out_specs=[whole, whole],
        out_shape=[pltpu.VMEM((2 * width, depth), BF16), pltpu.VMEM((depth, 2 * width), BF16)],
        scratch_shapes=[
            pltpu.VMEM(encoder.shape, BF16),
            pltpu.VMEM(decoder.shape, BF16),
            pltpu.SemaphoreType.DMA((2,)),
        ],
        cost_estimate=cost(8 * size(encoder)),
        compiler_params=pltpu.CompilerParams(vmem_limit_bytes=LIMIT),
    )(
        *[pltpu.with_memory_space_constraint(array, pltpu.HBM) for array in (encoder, decoder)],
        *[
            pltpu.with_memory_space_constraint(array, pltpu.VMEM)
            for array in (encoder_other, decoder_other)
        ],
    )


def size(array):
    return array.size * array.dtype.itemsize


def cost(moved):
    return pl.CostEstimate(flops=0, bytes_accessed=moved, transcendentals=0)


def stage_kernel(*refs):
    half = (len(refs) - 1) // 2
    copies = [
        pltpu.make_async_copy(
            source, target if len(source.shape) > 1 else target.at[0], refs[-1].at[i]
        )
        for i, (source, target) in enumerate(zip(refs[:half], refs[half:-1]))
    ]
    for copy in copies:
        copy.start()
    for copy in copies:
        copy.wait()


def stage(*arrays):
    shapes = [array.shape if array.ndim > 1 else (1,) + array.shape for array in arrays]
    return pl.pallas_call(
        stage_kernel,
        in_specs=[pl.BlockSpec(memory_space=pltpu.HBM)] * len(arrays),
        out_specs=[pl.BlockSpec(memory_space=pltpu.VMEM)] * len(arrays),
        out_shape=[pltpu.VMEM(shape, array.dtype) for shape, array in zip(shapes, arrays)],
        scratch_shapes=[pltpu.SemaphoreType.DMA((len(arrays),))],
        cost_estimate=cost(2 * sum(size(array) for array in arrays)),
        compiler_params=pltpu.CompilerParams(vmem_limit_bytes=LIMIT),
    )(*[pltpu.with_memory_space_constraint(array, pltpu.HBM) for array in arrays])


def near(kernel, arrays, outs):
    whole = pl.BlockSpec(memory_space=pltpu.VMEM)
    return pl.pallas_call(
        kernel,
        in_specs=[whole] * len(arrays),
        out_specs=[whole] * len(outs),
        out_shape=[pltpu.VMEM(shape, dtype) for shape, dtype in outs],
        cost_estimate=cost(sum(size(array) for array in arrays)),
        compiler_params=pltpu.CompilerParams(vmem_limit_bytes=LIMIT),
    )(*[pltpu.with_memory_space_constraint(array, pltpu.VMEM) for array in arrays])


def after(first, array):
    return lax.optimization_barrier((first, array))[1]


def on_device(
    count, rows_in, active_ids, encoder_weight, encoder_bias, threshold, decoder_weight, decoder_bias
):
    width = encoder_weight.shape[1]
    me = lax.axis_index("latent")
    core = me & 1

    def swap(array, bit):
        return lax.ppermute(array, "latent", [(i, i ^ bit) for i in range(count)])

    hops = []
    bit = 2
    while bit < count:
        hops.append(bit)
        bit *= 2

    encoder_other = swap(encoder_weight, 1)
    decoder_other = swap(decoder_weight, 1)
    bias_other = swap(encoder_bias[None], 1)

    per_device, depth = rows_in.shape
    ids = active_ids.reshape(2, count // 4, 2, per_device, active_ids.shape[1])
    side = jnp.where((me & hops[-1]) == 0, 0, 1)

    def listed(half, part):
        one = lax.dynamic_index_in_dim(ids, half, 0, keepdims=False)
        one = lax.dynamic_index_in_dim(one, part, 1, keepdims=False)
        return one.reshape(count // 4 * per_device, -1)

    lists = jnp.concatenate([listed(side, core), listed(1 - side, core)])
    lists_other = jnp.concatenate([listed(side, 1 - core), listed(1 - side, 1 - core)])

    block, bias_row = stage(rows_in, decoder_bias)
    for bit in hops[:-1]:
        if bit == hops[-2]:
            weights = (encoder_weight, decoder_weight, encoder_bias)
            block, weights, lists = lax.optimization_barrier((block, weights, lists))
        other = swap(rows_in if bit == hops[0] else block, bit)
        low = jnp.concatenate([block, other], axis=0)
        high = jnp.concatenate([other, block], axis=0)
        block = jnp.where((me & bit) == 0, low, high)
    encoder_near, decoder_near, encoder_row = stage(*weights)
    block, encoder_near, decoder_near, encoder_row = lax.optimization_barrier(
        (block, encoder_near, decoder_near, encoder_row)
    )
    rows = block
    rows_far = swap(block, hops[-1])
    half_rows = rows.shape[0]

    def center(part):
        return (part.astype(F32) - bias_row).astype(BF16)

    gate_mine = opened(lists, me * width, width)
    gates = jnp.concatenate([gate_mine, opened(lists, (me ^ 1) * width, width)], axis=1)
    gates = gates.astype(F32)
    gates, gates_far = gates[:half_rows], gates[half_rows:]

    def forward(part, gate):
        return near(
            forward_kernel,
            (part, bias_row, gate, encoder_near, encoder_other, encoder_row, bias_other,
             decoder_near, decoder_other),
            (((half_rows, width), F32), ((half_rows, depth), BF16)),
        )

    preact_near, low = forward(rows, gates)
    preact_far, high = forward(after(low, rows_far), gates_far)
    every_row = jnp.concatenate([rows, after(high, rows_far)])
    rows_other = swap(every_row, 1)
    for bit in hops[:-1]:
        low, high_received = lax.optimization_barrier(low + swap(low, bit)), swap(high, bit)
        high = lax.optimization_barrier(high + after(low, high_received))
    high_received = swap(low, hops[-1])
    high, weights = lax.optimization_barrier((high, (encoder_weight, decoder_weight)))
    low_received = swap(high, hops[-1])
    encoder_turned, decoder_turned = turn(*weights, encoder_other, decoder_other)

    errors, part = near(
        backward_kernel,
        (low, low_received, rows, gates, high, high_received, rows_far, gates_far, bias_row,
         encoder_turned, decoder_turned),
        (((2 * half_rows, depth), BF16), ((1, depth), F32)),
    )
    errors_other = swap(errors, 1)
    part = part + swap(part, 1)
    errors_other, part = lax.optimization_barrier((errors_other, part))

    rows_other, lists_other, _ = lax.optimization_barrier((rows_other, lists_other, errors))
    centered_other = center(rows_other)
    gate_rest = opened(lists_other, me * width, width)
    preact_rest = dot(centered_other, encoder_weight) + encoder_bias
    preact = jnp.concatenate([preact_near, preact_far, preact_rest])
    gate = jnp.concatenate([gate_mine, gate_rest])
    every_centered = jnp.concatenate([center(every_row), centered_other])
    codes = jnp.where(gate, preact, 0.0).astype(BF16)

    every_error = jnp.concatenate([errors, errors_other])

    def small_outputs():
        code_grad = dot_last(every_error, decoder_weight)
        distance = (preact - threshold) / EPSILON
        kernel = jnp.exp(-0.5 * distance * distance) / (EPSILON * math.sqrt(2.0 * math.pi))
        grad_threshold = jnp.sum(-threshold * code_grad * kernel - SPARSITY * kernel, axis=0)
        preact_grad = jnp.where(gate, code_grad, 0.0)
        return grad_threshold, jnp.sum(preact_grad, axis=0), preact_grad.astype(BF16)

    def decoder_output():
        return dot_rows(codes, every_error).astype(BF16)

    def encoder_output():
        return dot_rows(every_centered, small[2]).astype(BF16)

    part = part + swap(part, hops[0])
    small, part = lax.optimization_barrier((small_outputs(), part))
    part = part + swap(part, hops[1])
    grad_decoder, part = lax.optimization_barrier((decoder_output(), part))
    (error_sum,) = near(sum_kernel, (errors, errors_other), (((1, depth), F32),))
    for bit in hops[2:]:
        part = part + swap(part, bit)
    grad_decoder_bias = (error_sum - part).reshape(depth)
    grad_encoder = encoder_output()
    grad_threshold, grad_encoder_bias, _ = small
    return (grad_encoder, grad_encoder_bias, grad_threshold, grad_decoder, grad_decoder_bias)


def solution(mesh):
    count = mesh.shape["latent"]

    def body(*args):
        return on_device(count, *args)

    placed = (
        P(("group", "latent"), None),
        P("group", None),
        P("group", "latent"),
        P(("group", "latent")),
        P(("group", "latent")),
        P(("group", "latent"), None),
        P("group"),
    )
    return jax.shard_map(
        body,
        mesh=mesh,
        in_specs=placed,
        out_specs=(
            P("group", "latent"),
            P(("group", "latent")),
            P(("group", "latent")),
            P(("group", "latent"), None),
            P("group"),
        ),
        check_vma=False,
    )
```

```python
import math

import jax
import jax.numpy as jnp
from jax import lax
from jax.experimental import pallas as pl
from jax.experimental.pallas import tpu as pltpu
from jax.sharding import PartitionSpec as P

EPSILON = 0.5
SPARSITY = 0.5
F32 = jnp.float32
BF16 = jnp.bfloat16
LIMIT = 12 * 1024 * 1024


def opened(ids, offset, width):
    latent = offset + lax.broadcasted_iota(jnp.int32, (1, 1, width), 2)
    return jnp.any(ids[:, :, None] == latent, axis=1)


def dot(a, b):
    return jnp.dot(a, b, preferred_element_type=F32)


def dot_last(a, b):
    return lax.dot_general(a, b, (((1,), (1,)), ((), ())), preferred_element_type=F32)


def dot_rows(a, b):
    return lax.dot_general(a, b, (((0,), (0,)), ((), ())), preferred_element_type=F32)


def forward_kernel(
    rows, decoder_bias, gates, encoder, encoder_other, bias, bias_other, decoder, decoder_other,
    preact, partial
):
    width = encoder.shape[1]
    centered = (rows[...].astype(F32) - decoder_bias[...]).astype(BF16)
    mine = dot(centered, encoder[...]) + bias[...]
    other = dot(centered, encoder_other[...]) + bias_other[...]
    preact[...] = mine
    codes = (mine * gates[:, :width]).astype(BF16)
    codes_other = (other * gates[:, width:]).astype(BF16)
    partial[...] = (dot(codes, decoder[...]) + dot(codes_other, decoder_other[...])).astype(BF16)


def backward_kernel(
    low, low_received, rows, gates, high, high_received, rows_far, gates_far, decoder_bias,
    encoder_turned, decoder_turned, errors, part
):
    def error(total, received, block):
        total = total[...].astype(F32) + received[...].astype(F32)
        return total + decoder_bias[...] - block[...].astype(F32)

    found = jnp.concatenate(
        [error(low, low_received, rows), error(high, high_received, rows_far)], axis=0
    ).astype(BF16)
    errors[...] = found
    gate = jnp.concatenate([gates[...], gates_far[...]], axis=0)
    width = gate.shape[1] // 2
    mine, other = dot(found, decoder_turned[:, :width]), dot(found, decoder_turned[:, width:])
    code_grad = jnp.concatenate([mine, other], axis=1)
    grad = jnp.sum(code_grad * gate, axis=0, keepdims=True)
    upper = grad.astype(BF16).astype(F32)
    row = lax.broadcasted_iota(jnp.int32, (8, grad.shape[1]), 0)
    both = jnp.where(row == 0, upper, jnp.where(row == 1, grad - upper, 0.0))
    spread = dot(both.astype(BF16), encoder_turned[...])
    part[...] = spread[0:1, :] + spread[1:2, :]


def sum_kernel(errors, errors_other, total):
    half = errors.shape[0] // 2

    def summed(ref):
        block = ref[...].astype(F32)
        first = jnp.sum(block[:half], axis=0, keepdims=True)
        return first + jnp.sum(block[half:], axis=0, keepdims=True)

    total[...] = summed(errors) + summed(errors_other)


def turn_kernel(
    encoder_far, decoder_far, encoder_other, decoder_other, encoder_turned, decoder_turned,
    encoder, decoder, ready
):
    first = pltpu.make_async_copy(decoder_far, decoder, ready.at[0])
    second = pltpu.make_async_copy(encoder_far, encoder, ready.at[1])
    first.start()
    second.start()
    width = encoder_other.shape[1]
    decoder_turned[:, width:] = decoder_other[...].T
    encoder_turned[width:, :] = encoder_other[...].T
    first.wait()
    decoder_turned[:, :width] = decoder[...].T
    second.wait()
    encoder_turned[:width, :] = encoder[...].T


def turn(encoder, decoder, encoder_other, decoder_other):
    depth, width = encoder.shape
    far = pl.BlockSpec(memory_space=pltpu.HBM)
    whole = pl.BlockSpec(memory_space=pltpu.VMEM)
    return pl.pallas_call(
        turn_kernel,
        in_specs=[far, far, whole, whole],
        out_specs=[whole, whole],
        out_shape=[pltpu.VMEM((2 * width, depth), BF16), pltpu.VMEM((depth, 2 * width), BF16)],
        scratch_shapes=[
            pltpu.VMEM(encoder.shape, BF16),
            pltpu.VMEM(decoder.shape, BF16),
            pltpu.SemaphoreType.DMA((2,)),
        ],
        cost_estimate=cost(8 * size(encoder)),
        compiler_params=pltpu.CompilerParams(vmem_limit_bytes=LIMIT),
    )(
        *[pltpu.with_memory_space_constraint(array, pltpu.HBM) for array in (encoder, decoder)],
        *[
            pltpu.with_memory_space_constraint(array, pltpu.VMEM)
            for array in (encoder_other, decoder_other)
        ],
    )


def size(array):
    return array.size * array.dtype.itemsize


def cost(moved):
    return pl.CostEstimate(flops=0, bytes_accessed=moved, transcendentals=0)


def stage_kernel(*refs):
    half = (len(refs) - 1) // 2
    copies = [
        pltpu.make_async_copy(
            source, target if len(source.shape) > 1 else target.at[0], refs[-1].at[i]
        )
        for i, (source, target) in enumerate(zip(refs[:half], refs[half:-1]))
    ]
    for copy in copies:
        copy.start()
    for copy in copies:
        copy.wait()


def stage(*arrays):
    shapes = [array.shape if array.ndim > 1 else (1,) + array.shape for array in arrays]
    return pl.pallas_call(
        stage_kernel,
        in_specs=[pl.BlockSpec(memory_space=pltpu.HBM)] * len(arrays),
        out_specs=[pl.BlockSpec(memory_space=pltpu.VMEM)] * len(arrays),
        out_shape=[pltpu.VMEM(shape, array.dtype) for shape, array in zip(shapes, arrays)],
        scratch_shapes=[pltpu.SemaphoreType.DMA((len(arrays),))],
        cost_estimate=cost(2 * sum(size(array) for array in arrays)),
        compiler_params=pltpu.CompilerParams(vmem_limit_bytes=LIMIT),
    )(*[pltpu.with_memory_space_constraint(array, pltpu.HBM) for array in arrays])


def near(kernel, arrays, outs):
    whole = pl.BlockSpec(memory_space=pltpu.VMEM)
    return pl.pallas_call(
        kernel,
        in_specs=[whole] * len(arrays),
        out_specs=[whole] * len(outs),
        out_shape=[pltpu.VMEM(shape, dtype) for shape, dtype in outs],
        cost_estimate=cost(sum(size(array) for array in arrays)),
        compiler_params=pltpu.CompilerParams(vmem_limit_bytes=LIMIT),
    )(*[pltpu.with_memory_space_constraint(array, pltpu.VMEM) for array in arrays])


def after(first, array):
    return lax.optimization_barrier((first, array))[1]


def on_device(
    count, rows_in, active_ids, encoder_weight, encoder_bias, threshold, decoder_weight, decoder_bias
):
    width = encoder_weight.shape[1]
    me = lax.axis_index("latent")
    core = me & 1

    def swap(array, bit):
        return lax.ppermute(array, "latent", [(i, i ^ bit) for i in range(count)])

    hops = []
    bit = 2
    while bit < count:
        hops.append(bit)
        bit *= 2

    encoder_other = swap(encoder_weight, 1)
    decoder_other = swap(decoder_weight, 1)
    bias_other = swap(encoder_bias[None], 1)

    per_device, depth = rows_in.shape
    slots = count // 4
    side = jnp.where((me & hops[-1]) == 0, 0, 1)

    block, bias_row, ids = stage(rows_in, decoder_bias, active_ids)
    for bit in hops[:-1]:
        if bit == hops[-2]:
            weights = (encoder_weight, decoder_weight, encoder_bias)
            block, weights = lax.optimization_barrier((block, weights))
        other = swap(rows_in if bit == hops[0] else block, bit)
        low = jnp.concatenate([block, other], axis=0)
        high = jnp.concatenate([other, block], axis=0)
        block = jnp.where((me & bit) == 0, low, high)
    encoder_near, decoder_near, encoder_row = stage(*weights)
    block, ids, encoder_near, decoder_near, encoder_row = lax.optimization_barrier(
        (block, ids, encoder_near, decoder_near, encoder_row)
    )
    rows = block
    rows_far = swap(block, hops[-1])
    half_rows = rows.shape[0]

    def quarter(half, part):
        firsts = [((half * slots + slot) * 2 + part) * per_device for slot in range(slots)]
        return jnp.concatenate([ids[first : first + per_device] for first in firsts])

    quarters = [[quarter(half, part) for part in range(2)] for half in range(2)]

    def listed(half, part):
        near, far = [jnp.where(part == 0, *pair) for pair in quarters]
        return jnp.where(half == 0, near, far)

    lists = jnp.concatenate([listed(side, core), listed(1 - side, core)])
    lists_other = jnp.concatenate([listed(side, 1 - core), listed(1 - side, 1 - core)])

    def center(part):
        return (part.astype(F32) - bias_row).astype(BF16)

    gate_mine = opened(lists, me * width, width)
    gates = jnp.concatenate([gate_mine, opened(lists, (me ^ 1) * width, width)], axis=1)
    gates = gates.astype(F32)
    gates, gates_far = gates[:half_rows], gates[half_rows:]

    def forward(part, gate):
        return near(
            forward_kernel,
            (part, bias_row, gate, encoder_near, encoder_other, encoder_row, bias_other,
             decoder_near, decoder_other),
            (((half_rows, width), F32), ((half_rows, depth), BF16)),
        )

    preact_near, low = forward(rows, gates)
    preact_far, high = forward(after(low, rows_far), gates_far)
    every_row = jnp.concatenate([rows, after(high, rows_far)])
    rows_other = swap(every_row, 1)
    for bit in hops[:-1]:
        low, high_received = lax.optimization_barrier(low + swap(low, bit)), swap(high, bit)
        high = lax.optimization_barrier(high + after(low, high_received))
    high_received = swap(low, hops[-1])
    high, weights = lax.optimization_barrier((high, (encoder_weight, decoder_weight)))
    low_received = swap(high, hops[-1])
    encoder_turned, decoder_turned = turn(*weights, encoder_other, decoder_other)

    errors, part = near(
        backward_kernel,
        (low, low_received, rows, gates, high, high_received, rows_far, gates_far, bias_row,
         encoder_turned, decoder_turned),
        (((2 * half_rows, depth), BF16), ((1, depth), F32)),
    )
    errors_other = swap(errors, 1)
    part = part + swap(part, 1)
    errors_other, part = lax.optimization_barrier((errors_other, part))

    rows_other, lists_other, threshold, _ = lax.optimization_barrier(
        (rows_other, lists_other, threshold, errors)
    )
    centered_other = center(rows_other)
    gate_rest = opened(lists_other, me * width, width)
    preact_rest = dot(centered_other, encoder_weight) + encoder_bias
    preact = jnp.concatenate([preact_near, preact_far, preact_rest])
    gate = jnp.concatenate([gate_mine, gate_rest])
    every_centered = jnp.concatenate([center(every_row), centered_other])
    codes = jnp.where(gate, preact, 0.0).astype(BF16)

    every_error = jnp.concatenate([errors, errors_other])

    def small_outputs():
        code_grad = dot_last(every_error, decoder_weight)
        distance = (preact - threshold) / EPSILON
        kernel = jnp.exp(-0.5 * distance * distance) / (EPSILON * math.sqrt(2.0 * math.pi))
        grad_threshold = jnp.sum(-threshold * code_grad * kernel - SPARSITY * kernel, axis=0)
        preact_grad = jnp.where(gate, code_grad, 0.0)
        return grad_threshold, jnp.sum(preact_grad, axis=0), preact_grad.astype(BF16)

    def decoder_output():
        return dot_rows(codes, every_error).astype(BF16)

    def encoder_output():
        return dot_rows(every_centered, small[2]).astype(BF16)

    part = part + swap(part, hops[0] | 1)
    small, part = lax.optimization_barrier((small_outputs(), part))
    part = part + swap(part, hops[1] | 1)
    grad_decoder, part = lax.optimization_barrier((decoder_output(), part))
    (error_sum,) = near(sum_kernel, (errors, errors_other), (((1, depth), F32),))
    for bit in hops[2:]:
        part = part + swap(part, bit | 1)
    grad_decoder_bias = (error_sum - part).reshape(depth)
    grad_encoder = encoder_output()
    grad_threshold, grad_encoder_bias, _ = small
    return (grad_encoder, grad_encoder_bias, grad_threshold, grad_decoder, grad_decoder_bias)


def solution(mesh):
    count = mesh.shape["latent"]

    def body(*args):
        return on_device(count, *args)

    placed = (
        P(("group", "latent"), None),
        P("group", None),
        P("group", "latent"),
        P(("group", "latent")),
        P(("group", "latent")),
        P(("group", "latent"), None),
        P("group"),
    )
    return jax.shard_map(
        body,
        mesh=mesh,
        in_specs=placed,
        out_specs=(
            P("group", "latent"),
            P(("group", "latent")),
            P(("group", "latent")),
            P(("group", "latent"), None),
            P("group"),
        ),
        check_vma=False,
    )
```

```python
import math

import jax
import jax.numpy as jnp
from jax import lax
from jax.experimental import pallas as pl
from jax.experimental.pallas import tpu as pltpu
from jax.sharding import PartitionSpec as P

EPSILON = 0.5
SPARSITY = 0.5
F32 = jnp.float32
BF16 = jnp.bfloat16
LIMIT = 12 * 1024 * 1024


def opened(ids, offset, width):
    latent = offset + lax.broadcasted_iota(jnp.int32, (1, 1, width), 2)
    return jnp.any(ids[:, :, None] == latent, axis=1)


def dot(a, b):
    return jnp.dot(a, b, preferred_element_type=F32)


def dot_last(a, b):
    return lax.dot_general(a, b, (((1,), (1,)), ((), ())), preferred_element_type=F32)


def dot_rows(a, b):
    return lax.dot_general(a, b, (((0,), (0,)), ((), ())), preferred_element_type=F32)


def forward_kernel(
    rows, decoder_bias, gates, encoder, encoder_other, bias, bias_other, decoder, decoder_other,
    preact, partial
):
    width = encoder.shape[1]
    centered = (rows[...].astype(F32) - decoder_bias[...]).astype(BF16)
    mine = dot(centered, encoder[...]) + bias[...]
    other = dot(centered, encoder_other[...]) + bias_other[...]
    preact[...] = mine
    codes = (mine * gates[:, :width]).astype(BF16)
    codes_other = (other * gates[:, width:]).astype(BF16)
    partial[...] = (dot(codes, decoder[...]) + dot(codes_other, decoder_other[...])).astype(BF16)


def backward_kernel(
    low, low_received, rows, gates, high, high_received, rows_far, gates_far, decoder_bias,
    encoder_turned, decoder_turned, errors, part
):
    def error(total, received, block):
        total = total[...].astype(F32) + received[...].astype(F32)
        return total + decoder_bias[...] - block[...].astype(F32)

    found = jnp.concatenate(
        [error(low, low_received, rows), error(high, high_received, rows_far)], axis=0
    ).astype(BF16)
    errors[...] = found
    gate = jnp.concatenate([gates[...], gates_far[...]], axis=0)
    width = gate.shape[1] // 2
    mine, other = dot(found, decoder_turned[:, :width]), dot(found, decoder_turned[:, width:])
    code_grad = jnp.concatenate([mine, other], axis=1)
    grad = jnp.sum(code_grad * gate, axis=0, keepdims=True)
    upper = grad.astype(BF16).astype(F32)
    row = lax.broadcasted_iota(jnp.int32, (8, grad.shape[1]), 0)
    both = jnp.where(row == 0, upper, jnp.where(row == 1, grad - upper, 0.0))
    spread = dot(both.astype(BF16), encoder_turned[...])
    part[...] = spread[0:1, :] + spread[1:2, :]


def sum_kernel(errors, errors_other, total):
    half = errors.shape[0] // 2

    def summed(ref):
        block = ref[...].astype(F32)
        first = jnp.sum(block[:half], axis=0, keepdims=True)
        return first + jnp.sum(block[half:], axis=0, keepdims=True)

    total[...] = summed(errors) + summed(errors_other)


def turn_kernel(
    encoder_far, decoder_far, encoder_other, decoder_other, encoder_turned, decoder_turned,
    encoder, decoder, ready
):
    first = pltpu.make_async_copy(decoder_far, decoder, ready.at[0])
    second = pltpu.make_async_copy(encoder_far, encoder, ready.at[1])
    first.start()
    second.start()
    width = encoder_other.shape[1]
    decoder_turned[:, width:] = decoder_other[...].T
    encoder_turned[width:, :] = encoder_other[...].T
    first.wait()
    decoder_turned[:, :width] = decoder[...].T
    second.wait()
    encoder_turned[:width, :] = encoder[...].T


def turn(encoder, decoder, encoder_other, decoder_other):
    depth, width = encoder.shape
    far = pl.BlockSpec(memory_space=pltpu.HBM)
    whole = pl.BlockSpec(memory_space=pltpu.VMEM)
    return pl.pallas_call(
        turn_kernel,
        in_specs=[far, far, whole, whole],
        out_specs=[whole, whole],
        out_shape=[pltpu.VMEM((2 * width, depth), BF16), pltpu.VMEM((depth, 2 * width), BF16)],
        scratch_shapes=[
            pltpu.VMEM(encoder.shape, BF16),
            pltpu.VMEM(decoder.shape, BF16),
            pltpu.SemaphoreType.DMA((2,)),
        ],
        cost_estimate=cost(8 * size(encoder)),
        compiler_params=pltpu.CompilerParams(vmem_limit_bytes=LIMIT),
    )(
        *[pltpu.with_memory_space_constraint(array, pltpu.HBM) for array in (encoder, decoder)],
        *[
            pltpu.with_memory_space_constraint(array, pltpu.VMEM)
            for array in (encoder_other, decoder_other)
        ],
    )


def size(array):
    return array.size * array.dtype.itemsize


def cost(moved):
    return pl.CostEstimate(flops=0, bytes_accessed=moved, transcendentals=0)


def stage_kernel(*refs):
    half = (len(refs) - 1) // 2
    copies = [
        pltpu.make_async_copy(
            source, target if len(source.shape) > 1 else target.at[0], refs[-1].at[i]
        )
        for i, (source, target) in enumerate(zip(refs[:half], refs[half:-1]))
    ]
    for copy in copies:
        copy.start()
    for copy in copies:
        copy.wait()


def stage(*arrays):
    shapes = [array.shape if array.ndim > 1 else (1,) + array.shape for array in arrays]
    return pl.pallas_call(
        stage_kernel,
        in_specs=[pl.BlockSpec(memory_space=pltpu.HBM)] * len(arrays),
        out_specs=[pl.BlockSpec(memory_space=pltpu.VMEM)] * len(arrays),
        out_shape=[pltpu.VMEM(shape, array.dtype) for shape, array in zip(shapes, arrays)],
        scratch_shapes=[pltpu.SemaphoreType.DMA((len(arrays),))],
        cost_estimate=cost(2 * sum(size(array) for array in arrays)),
        compiler_params=pltpu.CompilerParams(vmem_limit_bytes=LIMIT),
    )(*[pltpu.with_memory_space_constraint(array, pltpu.HBM) for array in arrays])


def near(kernel, arrays, outs):
    whole = pl.BlockSpec(memory_space=pltpu.VMEM)
    return pl.pallas_call(
        kernel,
        in_specs=[whole] * len(arrays),
        out_specs=[whole] * len(outs),
        out_shape=[pltpu.VMEM(shape, dtype) for shape, dtype in outs],
        cost_estimate=cost(sum(size(array) for array in arrays)),
        compiler_params=pltpu.CompilerParams(vmem_limit_bytes=LIMIT),
    )(*[pltpu.with_memory_space_constraint(array, pltpu.VMEM) for array in arrays])


def after(first, array):
    return lax.optimization_barrier((first, array))[1]


def on_device(
    count, rows_in, active_ids, encoder_weight, encoder_bias, threshold, decoder_weight, decoder_bias
):
    width = encoder_weight.shape[1]
    me = lax.axis_index("latent")

    def swap(array, bit):
        return lax.ppermute(array, "latent", [(i, i ^ bit) for i in range(count)])

    hops = []
    bit = 2
    while bit < count:
        hops.append(bit)
        bit *= 2
    gathering = hops[1:] + hops[:1]

    encoder_other = swap(encoder_weight, 1)
    decoder_other = swap(decoder_weight, 1)
    bias_other = swap(encoder_bias[None], 1)

    per_device, depth = rows_in.shape
    slots = count // 4
    kind = me & 1
    for bit in hops:
        kind = kind ^ jnp.where((me & bit) == 0, 0, 1)
    side = jnp.where((me & gathering[-1]) == 0, 0, 1)

    block, bias_row, ids = stage(rows_in, decoder_bias, active_ids)
    for bit in gathering[:-1]:
        if bit == gathering[-2]:
            weights = (encoder_weight, decoder_weight, encoder_bias)
            block, weights = lax.optimization_barrier((block, weights))
        other = swap(rows_in if bit == gathering[0] else block, bit | 1)
        low = jnp.concatenate([block, other], axis=0)
        high = jnp.concatenate([other, block], axis=0)
        block = jnp.where((me & bit) == 0, low, high)
    encoder_near, decoder_near, encoder_row = stage(*weights)
    block, ids, encoder_near, decoder_near, encoder_row = lax.optimization_barrier(
        (block, ids, encoder_near, decoder_near, encoder_row)
    )
    rows = block
    rows_far = swap(block, gathering[-1] | 1)
    half_rows = rows.shape[0]

    def quarter(half, kind):
        lines = []
        for slot in range(slots):
            first = (slot * 2 + half) * 2
            first += (bin(first).count("1") + kind) % 2
            lines.append(ids[first * per_device : (first + 1) * per_device])
        return jnp.concatenate(lines)

    quarters = [[quarter(half, kind) for kind in range(2)] for half in range(2)]

    def listed(half, kind):
        near, far = [jnp.where(kind == 0, *pair) for pair in quarters]
        return jnp.where(half == 0, near, far)

    lists = jnp.concatenate([listed(side, kind), listed(1 - side, kind)])
    lists_other = jnp.concatenate([listed(side, 1 - kind), listed(1 - side, 1 - kind)])

    def center(part):
        return (part.astype(F32) - bias_row).astype(BF16)

    gate_mine = opened(lists, me * width, width)
    gates = jnp.concatenate([gate_mine, opened(lists, (me ^ 1) * width, width)], axis=1)
    gates = gates.astype(F32)
    gates, gates_far = gates[:half_rows], gates[half_rows:]

    def forward(part, gate):
        return near(
            forward_kernel,
            (part, bias_row, gate, encoder_near, encoder_other, encoder_row, bias_other,
             decoder_near, decoder_other),
            (((half_rows, width), F32), ((half_rows, depth), BF16)),
        )

    preact_near, low = forward(rows, gates)
    preact_far, high = forward(after(low, rows_far), gates_far)
    every_row = jnp.concatenate([rows, after(high, rows_far)])
    rows_other = swap(every_row, 1)
    for bit in gathering[:-1]:
        low, high_received = lax.optimization_barrier(low + swap(low, bit | 1)), swap(high, bit | 1)
        high = lax.optimization_barrier(high + after(low, high_received))
    high_received = swap(low, gathering[-1] | 1)
    high, weights = lax.optimization_barrier((high, (encoder_weight, decoder_weight)))
    low_received = swap(high, gathering[-1] | 1)
    encoder_turned, decoder_turned = turn(*weights, encoder_other, decoder_other)

    errors, part = near(
        backward_kernel,
        (low, low_received, rows, gates, high, high_received, rows_far, gates_far, bias_row,
         encoder_turned, decoder_turned),
        (((2 * half_rows, depth), BF16), ((1, depth), F32)),
    )
    errors_other = swap(errors, 1)
    part = part + swap(part, 1)
    errors_other, part = lax.optimization_barrier((errors_other, part))

    rows_other, lists_other, threshold, _ = lax.optimization_barrier(
        (rows_other, lists_other, threshold, errors)
    )
    centered_other = center(rows_other)
    gate_rest = opened(lists_other, me * width, width)
    preact_rest = dot(centered_other, encoder_weight) + encoder_bias
    preact = jnp.concatenate([preact_near, preact_far, preact_rest])
    gate = jnp.concatenate([gate_mine, gate_rest])
    every_centered = jnp.concatenate([center(every_row), centered_other])
    codes = jnp.where(gate, preact, 0.0).astype(BF16)

    every_error = jnp.concatenate([errors, errors_other])

    def small_outputs():
        code_grad = dot_last(every_error, decoder_weight)
        distance = (preact - threshold) / EPSILON
        kernel = jnp.exp(-0.5 * distance * distance) / (EPSILON * math.sqrt(2.0 * math.pi))
        grad_threshold = jnp.sum(-threshold * code_grad * kernel - SPARSITY * kernel, axis=0)
        preact_grad = jnp.where(gate, code_grad, 0.0)
        return grad_threshold, jnp.sum(preact_grad, axis=0), preact_grad.astype(BF16)

    def decoder_output():
        return dot_rows(codes, every_error).astype(BF16)

    def encoder_output():
        return dot_rows(every_centered, small[2]).astype(BF16)

    part = part + swap(part, hops[0] | 1)
    small, part = lax.optimization_barrier((small_outputs(), part))
    part = part + swap(part, hops[1] | 1)
    grad_decoder, part = lax.optimization_barrier((decoder_output(), part))
    (error_sum,) = near(sum_kernel, (errors, errors_other), (((1, depth), F32),))
    for bit in hops[2:]:
        part = part + swap(part, bit | 1)
    grad_decoder_bias = (error_sum - part).reshape(depth)
    grad_encoder = encoder_output()
    grad_threshold, grad_encoder_bias, _ = small
    return (grad_encoder, grad_encoder_bias, grad_threshold, grad_decoder, grad_decoder_bias)


def solution(mesh):
    count = mesh.shape["latent"]

    def body(*args):
        return on_device(count, *args)

    placed = (
        P(("group", "latent"), None),
        P("group", None),
        P("group", "latent"),
        P(("group", "latent")),
        P(("group", "latent")),
        P(("group", "latent"), None),
        P("group"),
    )
    return jax.shard_map(
        body,
        mesh=mesh,
        in_specs=placed,
        out_specs=(
            P("group", "latent"),
            P(("group", "latent")),
            P(("group", "latent")),
            P(("group", "latent"), None),
            P("group"),
        ),
        check_vma=False,
    )
```

```python
import math

import jax
import jax.numpy as jnp
from jax import lax
from jax.experimental import pallas as pl
from jax.experimental.pallas import tpu as pltpu
from jax.sharding import PartitionSpec as P

EPSILON = 0.5
SPARSITY = 0.5
F32 = jnp.float32
BF16 = jnp.bfloat16
LIMIT = 12 * 1024 * 1024


def opened(ids, offset, width):
    latent = offset + lax.broadcasted_iota(jnp.int32, (1, 1, width), 2)
    return jnp.any(ids[:, :, None] == latent, axis=1)


def dot(a, b):
    return jnp.dot(a, b, preferred_element_type=F32)


def dot_last(a, b):
    return lax.dot_general(a, b, (((1,), (1,)), ((), ())), preferred_element_type=F32)


def dot_rows(a, b):
    return lax.dot_general(a, b, (((0,), (0,)), ((), ())), preferred_element_type=F32)


def forward_kernel(
    rows, decoder_bias, gates, encoder, encoder_other, bias, bias_other, decoder, decoder_other,
    preact, partial
):
    width = encoder.shape[1]
    centered = (rows[...].astype(F32) - decoder_bias[...]).astype(BF16)
    mine = dot(centered, encoder[...]) + bias[...]
    other = dot(centered, encoder_other[...]) + bias_other[...]
    preact[...] = mine
    codes = (mine * gates[:, :width]).astype(BF16)
    codes_other = (other * gates[:, width:]).astype(BF16)
    partial[...] = (dot(codes, decoder[...]) + dot(codes_other, decoder_other[...])).astype(BF16)


def backward_kernel(
    low, low_received, rows, gates, high, high_received, rows_far, gates_far, decoder_bias,
    encoder_turned, decoder_turned, errors, part
):
    def error(total, received, block):
        total = total[...].astype(F32) + received[...].astype(F32)
        return total + decoder_bias[...] - block[...].astype(F32)

    found = jnp.concatenate(
        [error(low, low_received, rows), error(high, high_received, rows_far)], axis=0
    ).astype(BF16)
    errors[...] = found
    gate = jnp.concatenate([gates[...], gates_far[...]], axis=0)
    width = gate.shape[1] // 2
    mine, other = dot(found, decoder_turned[:, :width]), dot(found, decoder_turned[:, width:])
    code_grad = jnp.concatenate([mine, other], axis=1)
    grad = jnp.sum(code_grad * gate, axis=0, keepdims=True)
    upper = grad.astype(BF16).astype(F32)
    row = lax.broadcasted_iota(jnp.int32, (8, grad.shape[1]), 0)
    both = jnp.where(row == 0, upper, jnp.where(row == 1, grad - upper, 0.0))
    spread = dot(both.astype(BF16), encoder_turned[...])
    part[...] = spread[0:1, :] + spread[1:2, :]


def sum_kernel(errors, errors_other, total):
    half = errors.shape[0] // 2

    def summed(ref):
        block = ref[...].astype(F32)
        first = jnp.sum(block[:half], axis=0, keepdims=True)
        return first + jnp.sum(block[half:], axis=0, keepdims=True)

    total[...] = summed(errors) + summed(errors_other)


def turn_kernel(
    encoder_far, decoder_far, encoder_other, decoder_other, encoder_turned, decoder_turned,
    encoder, decoder, ready
):
    first = pltpu.make_async_copy(decoder_far, decoder, ready.at[0])
    second = pltpu.make_async_copy(encoder_far, encoder, ready.at[1])
    first.start()
    second.start()
    width = encoder_other.shape[1]
    decoder_turned[:, width:] = decoder_other[...].T
    encoder_turned[width:, :] = encoder_other[...].T
    first.wait()
    decoder_turned[:, :width] = decoder[...].T
    second.wait()
    encoder_turned[:width, :] = encoder[...].T


def turn(encoder, decoder, encoder_other, decoder_other):
    depth, width = encoder.shape
    far = pl.BlockSpec(memory_space=pltpu.HBM)
    whole = pl.BlockSpec(memory_space=pltpu.VMEM)
    return pl.pallas_call(
        turn_kernel,
        in_specs=[far, far, whole, whole],
        out_specs=[whole, whole],
        out_shape=[pltpu.VMEM((2 * width, depth), BF16), pltpu.VMEM((depth, 2 * width), BF16)],
        scratch_shapes=[
            pltpu.VMEM(encoder.shape, BF16),
            pltpu.VMEM(decoder.shape, BF16),
            pltpu.SemaphoreType.DMA((2,)),
        ],
        cost_estimate=cost(8 * size(encoder)),
        compiler_params=pltpu.CompilerParams(vmem_limit_bytes=LIMIT),
    )(
        *[pltpu.with_memory_space_constraint(array, pltpu.HBM) for array in (encoder, decoder)],
        *[
            pltpu.with_memory_space_constraint(array, pltpu.VMEM)
            for array in (encoder_other, decoder_other)
        ],
    )


def size(array):
    return array.size * array.dtype.itemsize


def cost(moved):
    return pl.CostEstimate(flops=0, bytes_accessed=moved, transcendentals=0)


def stage_kernel(*refs):
    half = (len(refs) - 1) // 2
    copies = [
        pltpu.make_async_copy(
            source, target if len(source.shape) > 1 else target.at[0], refs[-1].at[i]
        )
        for i, (source, target) in enumerate(zip(refs[:half], refs[half:-1]))
    ]
    for copy in copies:
        copy.start()
    for copy in copies:
        copy.wait()


def stage(*arrays):
    shapes = [array.shape if array.ndim > 1 else (1,) + array.shape for array in arrays]
    return pl.pallas_call(
        stage_kernel,
        in_specs=[pl.BlockSpec(memory_space=pltpu.HBM)] * len(arrays),
        out_specs=[pl.BlockSpec(memory_space=pltpu.VMEM)] * len(arrays),
        out_shape=[pltpu.VMEM(shape, array.dtype) for shape, array in zip(shapes, arrays)],
        scratch_shapes=[pltpu.SemaphoreType.DMA((len(arrays),))],
        cost_estimate=cost(2 * sum(size(array) for array in arrays)),
        compiler_params=pltpu.CompilerParams(vmem_limit_bytes=LIMIT),
    )(*[pltpu.with_memory_space_constraint(array, pltpu.HBM) for array in arrays])


def near(kernel, arrays, outs):
    whole = pl.BlockSpec(memory_space=pltpu.VMEM)
    return pl.pallas_call(
        kernel,
        in_specs=[whole] * len(arrays),
        out_specs=[whole] * len(outs),
        out_shape=[pltpu.VMEM(shape, dtype) for shape, dtype in outs],
        cost_estimate=cost(sum(size(array) for array in arrays)),
        compiler_params=pltpu.CompilerParams(vmem_limit_bytes=LIMIT),
    )(*[pltpu.with_memory_space_constraint(array, pltpu.VMEM) for array in arrays])


def after(first, array):
    return lax.optimization_barrier((first, array))[1]


def on_device(
    count, rows_in, active_ids, encoder_weight, encoder_bias, threshold, decoder_weight, decoder_bias
):
    width = encoder_weight.shape[1]
    me = lax.axis_index("latent")

    def swap(array, bit):
        return lax.ppermute(array, "latent", [(i, i ^ bit) for i in range(count)])

    hops = []
    bit = 2
    while bit < count:
        hops.append(bit)
        bit *= 2
    gathering = hops[:0:-1] + hops[:1]

    encoder_other = swap(encoder_weight, 1)
    decoder_other = swap(decoder_weight, 1)
    bias_other = swap(encoder_bias[None], 1)

    per_device, depth = rows_in.shape
    slots = count // 4
    kind = me & 1
    for bit in hops:
        kind = kind ^ jnp.where((me & bit) == 0, 0, 1)
    side = jnp.where((me & gathering[-1]) == 0, 0, 1)

    block, bias_row, ids = stage(rows_in, decoder_bias, active_ids)
    for bit in gathering[:-1]:
        if bit == gathering[-2]:
            weights = (encoder_weight, decoder_weight, encoder_bias)
            block, weights = lax.optimization_barrier((block, weights))
        other = swap(rows_in if bit == gathering[0] else block, bit | 1)
        low = jnp.concatenate([block, other], axis=0)
        high = jnp.concatenate([other, block], axis=0)
        block = jnp.where((me & bit) == 0, low, high)
    encoder_near, decoder_near, encoder_row = stage(*weights)
    block, ids, encoder_near, decoder_near, encoder_row = lax.optimization_barrier(
        (block, ids, encoder_near, decoder_near, encoder_row)
    )
    rows = block
    rows_far = swap(block, gathering[-1] | 1)
    half_rows = rows.shape[0]

    def quarter(half, kind):
        lines = []
        for place in range(slots):
            slot = sum(slots // (2 << i) for i in range(slots.bit_length() - 1) if (place >> i) & 1)
            first = (slot * 2 + half) * 2
            first += (bin(first).count("1") + kind) % 2
            lines.append(ids[first * per_device : (first + 1) * per_device])
        return jnp.concatenate(lines)

    quarters = [[quarter(half, kind) for kind in range(2)] for half in range(2)]

    def listed(half, kind):
        near, far = [jnp.where(kind == 0, *pair) for pair in quarters]
        return jnp.where(half == 0, near, far)

    lists = jnp.concatenate([listed(side, kind), listed(1 - side, kind)])
    lists_other = jnp.concatenate([listed(side, 1 - kind), listed(1 - side, 1 - kind)])

    def center(part):
        return (part.astype(F32) - bias_row).astype(BF16)

    gate_mine = opened(lists, me * width, width)
    gates = jnp.concatenate([gate_mine, opened(lists, (me ^ 1) * width, width)], axis=1)
    gates = gates.astype(F32)
    gates, gates_far = gates[:half_rows], gates[half_rows:]

    def forward(part, gate):
        return near(
            forward_kernel,
            (part, bias_row, gate, encoder_near, encoder_other, encoder_row, bias_other,
             decoder_near, decoder_other),
            (((half_rows, width), F32), ((half_rows, depth), BF16)),
        )

    preact_near, low = forward(rows, gates)
    preact_far, high = forward(after(low, rows_far), gates_far)
    every_row = jnp.concatenate([rows, after(high, rows_far)])
    rows_other = swap(every_row, 1)
    for bit in gathering[-2::-1]:
        low, high_received = lax.optimization_barrier(low + swap(low, bit | 1)), swap(high, bit | 1)
        high = lax.optimization_barrier(high + after(low, high_received))
    high_received = swap(low, gathering[-1] | 1)
    high, weights = lax.optimization_barrier((high, (encoder_weight, decoder_weight)))
    low_received = swap(high, gathering[-1] | 1)
    encoder_turned, decoder_turned = turn(*weights, encoder_other, decoder_other)

    errors, part = near(
        backward_kernel,
        (low, low_received, rows, gates, high, high_received, rows_far, gates_far, bias_row,
         encoder_turned, decoder_turned),
        (((2 * half_rows, depth), BF16), ((1, depth), F32)),
    )
    errors_other = swap(errors, 1)
    part = part + swap(part, 1)
    errors_other, part = lax.optimization_barrier((errors_other, part))

    rows_other, lists_other, threshold, _ = lax.optimization_barrier(
        (rows_other, lists_other, threshold, errors)
    )
    centered_other = center(rows_other)
    gate_rest = opened(lists_other, me * width, width)
    preact_rest = dot(centered_other, encoder_weight) + encoder_bias
    preact = jnp.concatenate([preact_near, preact_far, preact_rest])
    gate = jnp.concatenate([gate_mine, gate_rest])
    every_centered = jnp.concatenate([center(every_row), centered_other])
    codes = jnp.where(gate, preact, 0.0).astype(BF16)

    every_error = jnp.concatenate([errors, errors_other])

    def small_outputs():
        code_grad = dot_last(every_error, decoder_weight)
        distance = (preact - threshold) / EPSILON
        kernel = jnp.exp(-0.5 * distance * distance) / (EPSILON * math.sqrt(2.0 * math.pi))
        grad_threshold = jnp.sum(-threshold * code_grad * kernel - SPARSITY * kernel, axis=0)
        preact_grad = jnp.where(gate, code_grad, 0.0)
        return grad_threshold, jnp.sum(preact_grad, axis=0), preact_grad.astype(BF16)

    def decoder_output():
        return dot_rows(codes, every_error).astype(BF16)

    def encoder_output():
        return dot_rows(every_centered, small[2]).astype(BF16)

    part = part + swap(part, hops[0] | 1)
    small, part = lax.optimization_barrier((small_outputs(), part))
    part = part + swap(part, hops[1] | 1)
    grad_decoder, part = lax.optimization_barrier((decoder_output(), part))
    (error_sum,) = near(sum_kernel, (errors, errors_other), (((1, depth), F32),))
    for bit in hops[2:]:
        part = part + swap(part, bit | 1)
    grad_decoder_bias = (error_sum - part).reshape(depth)
    grad_encoder = encoder_output()
    grad_threshold, grad_encoder_bias, _ = small
    return (grad_encoder, grad_encoder_bias, grad_threshold, grad_decoder, grad_decoder_bias)


def solution(mesh):
    count = mesh.shape["latent"]

    def body(*args):
        return on_device(count, *args)

    placed = (
        P(("group", "latent"), None),
        P("group", None),
        P("group", "latent"),
        P(("group", "latent")),
        P(("group", "latent")),
        P(("group", "latent"), None),
        P("group"),
    )
    return jax.shard_map(
        body,
        mesh=mesh,
        in_specs=placed,
        out_specs=(
            P("group", "latent"),
            P(("group", "latent")),
            P(("group", "latent")),
            P(("group", "latent"), None),
            P("group"),
        ),
        check_vma=False,
    )
```

```python
import math

import jax
import jax.numpy as jnp
from jax import lax
from jax.experimental import pallas as pl
from jax.experimental.pallas import tpu as pltpu
from jax.sharding import PartitionSpec as P

EPSILON = 0.5
SPARSITY = 0.5
F32 = jnp.float32
BF16 = jnp.bfloat16
LIMIT = 12 * 1024 * 1024


def opened(ids, offset, width):
    latent = offset + lax.broadcasted_iota(jnp.int32, (1, 1, width), 2)
    return jnp.any(ids[:, :, None] == latent, axis=1)


def dot(a, b):
    return jnp.dot(a, b, preferred_element_type=F32)


def dot_last(a, b):
    return lax.dot_general(a, b, (((1,), (1,)), ((), ())), preferred_element_type=F32)


def dot_rows(a, b):
    return lax.dot_general(a, b, (((0,), (0,)), ((), ())), preferred_element_type=F32)


def forward_kernel(
    rows, decoder_bias, gates, encoder, encoder_other, bias, bias_other, decoder, decoder_other,
    preact, partial
):
    width = encoder.shape[1]
    centered = (rows[...].astype(F32) - decoder_bias[...]).astype(BF16)
    mine = dot(centered, encoder[...]) + bias[...]
    other = dot(centered, encoder_other[...]) + bias_other[...]
    preact[...] = mine
    codes = (mine * gates[:, :width]).astype(BF16)
    codes_other = (other * gates[:, width:]).astype(BF16)
    partial[...] = (dot(codes, decoder[...]) + dot(codes_other, decoder_other[...])).astype(BF16)


def backward_kernel(
    low, low_received, rows, gates, high, high_received, rows_far, gates_far, decoder_bias,
    encoder_turned, decoder_turned, errors, part
):
    def error(total, received, block):
        total = total[...].astype(F32) + received[...].astype(F32)
        return total + decoder_bias[...] - block[...].astype(F32)

    found = jnp.concatenate(
        [error(low, low_received, rows), error(high, high_received, rows_far)], axis=0
    ).astype(BF16)
    errors[...] = found
    gate = jnp.concatenate([gates[...], gates_far[...]], axis=0)
    width = gate.shape[1] // 2
    mine, other = dot(found, decoder_turned[:, :width]), dot(found, decoder_turned[:, width:])
    code_grad = jnp.concatenate([mine, other], axis=1)
    grad = jnp.sum(code_grad * gate, axis=0, keepdims=True)
    upper = grad.astype(BF16).astype(F32)
    row = lax.broadcasted_iota(jnp.int32, (8, grad.shape[1]), 0)
    both = jnp.where(row == 0, upper, jnp.where(row == 1, grad - upper, 0.0))
    spread = dot(both.astype(BF16), encoder_turned[...])
    part[...] = spread[0:1, :] + spread[1:2, :]


def sum_kernel(errors, errors_other, total):
    half = errors.shape[0] // 2

    def summed(ref):
        block = ref[...].astype(F32)
        first = jnp.sum(block[:half], axis=0, keepdims=True)
        return first + jnp.sum(block[half:], axis=0, keepdims=True)

    total[...] = summed(errors) + summed(errors_other)


def turn_kernel(
    encoder_far, decoder_far, encoder_other, decoder_other, encoder_turned, decoder_turned,
    encoder, decoder, ready
):
    first = pltpu.make_async_copy(decoder_far, decoder, ready.at[0])
    second = pltpu.make_async_copy(encoder_far, encoder, ready.at[1])
    first.start()
    second.start()
    width = encoder_other.shape[1]
    decoder_turned[:, width:] = decoder_other[...].T
    encoder_turned[width:, :] = encoder_other[...].T
    first.wait()
    decoder_turned[:, :width] = decoder[...].T
    second.wait()
    encoder_turned[:width, :] = encoder[...].T


def turn(encoder, decoder, encoder_other, decoder_other):
    depth, width = encoder.shape
    far = pl.BlockSpec(memory_space=pltpu.HBM)
    whole = pl.BlockSpec(memory_space=pltpu.VMEM)
    return pl.pallas_call(
        turn_kernel,
        in_specs=[far, far, whole, whole],
        out_specs=[whole, whole],
        out_shape=[pltpu.VMEM((2 * width, depth), BF16), pltpu.VMEM((depth, 2 * width), BF16)],
        scratch_shapes=[
            pltpu.VMEM(encoder.shape, BF16),
            pltpu.VMEM(decoder.shape, BF16),
            pltpu.SemaphoreType.DMA((2,)),
        ],
        cost_estimate=cost(8 * size(encoder)),
        compiler_params=pltpu.CompilerParams(vmem_limit_bytes=LIMIT),
    )(
        *[pltpu.with_memory_space_constraint(array, pltpu.HBM) for array in (encoder, decoder)],
        *[
            pltpu.with_memory_space_constraint(array, pltpu.VMEM)
            for array in (encoder_other, decoder_other)
        ],
    )


def size(array):
    return array.size * array.dtype.itemsize


def cost(moved):
    return pl.CostEstimate(flops=0, bytes_accessed=moved, transcendentals=0)


def stage_kernel(*refs):
    half = (len(refs) - 1) // 2
    copies = [
        pltpu.make_async_copy(
            source, target if len(source.shape) > 1 else target.at[0], refs[-1].at[i]
        )
        for i, (source, target) in enumerate(zip(refs[:half], refs[half:-1]))
    ]
    for copy in copies:
        copy.start()
    for copy in copies:
        copy.wait()


def stage(*arrays):
    shapes = [array.shape if array.ndim > 1 else (1,) + array.shape for array in arrays]
    return pl.pallas_call(
        stage_kernel,
        in_specs=[pl.BlockSpec(memory_space=pltpu.HBM)] * len(arrays),
        out_specs=[pl.BlockSpec(memory_space=pltpu.VMEM)] * len(arrays),
        out_shape=[pltpu.VMEM(shape, array.dtype) for shape, array in zip(shapes, arrays)],
        scratch_shapes=[pltpu.SemaphoreType.DMA((len(arrays),))],
        cost_estimate=cost(2 * sum(size(array) for array in arrays)),
        compiler_params=pltpu.CompilerParams(vmem_limit_bytes=LIMIT),
    )(*[pltpu.with_memory_space_constraint(array, pltpu.HBM) for array in arrays])


def near(kernel, arrays, outs):
    whole = pl.BlockSpec(memory_space=pltpu.VMEM)
    return pl.pallas_call(
        kernel,
        in_specs=[whole] * len(arrays),
        out_specs=[whole] * len(outs),
        out_shape=[pltpu.VMEM(shape, dtype) for shape, dtype in outs],
        cost_estimate=cost(sum(size(array) for array in arrays)),
        compiler_params=pltpu.CompilerParams(vmem_limit_bytes=LIMIT),
    )(*[pltpu.with_memory_space_constraint(array, pltpu.VMEM) for array in arrays])


def after(first, array):
    return lax.optimization_barrier((first, array))[1]


def on_device(
    count, rows_in, active_ids, encoder_weight, encoder_bias, threshold, decoder_weight, decoder_bias
):
    width = encoder_weight.shape[1]
    me = lax.axis_index("latent")

    def swap(array, bit):
        return lax.ppermute(array, "latent", [(i, i ^ bit) for i in range(count)])

    hops = []
    bit = 2
    while bit < count:
        hops.append(bit)
        bit *= 2
    gathering = hops[:0:-1] + hops[:1]

    encoder_other = swap(encoder_weight, 1)
    bias_other = swap(encoder_bias[None], 1)

    per_device, depth = rows_in.shape
    slots = count // 4
    kind = me & 1
    for bit in hops:
        kind = kind ^ jnp.where((me & bit) == 0, 0, 1)
    side = jnp.where((me & gathering[-1]) == 0, 0, 1)

    block, bias_row, ids = stage(rows_in, decoder_bias, active_ids)
    for bit in gathering[:-1]:
        if bit == gathering[-2]:
            weights = (encoder_weight, decoder_weight, encoder_bias)
            block, weights = lax.optimization_barrier((block, weights))
            decoder_other = swap(weights[1], 1)
        other = swap(rows_in if bit == gathering[0] else block, bit | 1)
        low = jnp.concatenate([block, other], axis=0)
        high = jnp.concatenate([other, block], axis=0)
        block = jnp.where((me & bit) == 0, low, high)
    encoder_near, decoder_near, encoder_row = stage(*weights)
    block, ids, encoder_near, decoder_near, encoder_row = lax.optimization_barrier(
        (block, ids, encoder_near, decoder_near, encoder_row)
    )
    rows = block
    rows_far = swap(block, gathering[-1] | 1)
    half_rows = rows.shape[0]

    def quarter(half, kind):
        lines = []
        for place in range(slots):
            slot = sum(slots // (2 << i) for i in range(slots.bit_length() - 1) if (place >> i) & 1)
            first = (slot * 2 + half) * 2
            first += (bin(first).count("1") + kind) % 2
            lines.append(ids[first * per_device : (first + 1) * per_device])
        return jnp.concatenate(lines)

    quarters = [[quarter(half, kind) for kind in range(2)] for half in range(2)]

    def listed(half, kind):
        near, far = [jnp.where(kind == 0, *pair) for pair in quarters]
        return jnp.where(half == 0, near, far)

    lists = jnp.concatenate([listed(side, kind), listed(1 - side, kind)])
    lists_other = jnp.concatenate([listed(side, 1 - kind), listed(1 - side, 1 - kind)])

    def center(part):
        return (part.astype(F32) - bias_row).astype(BF16)

    gate_mine = opened(lists, me * width, width)
    gates = jnp.concatenate([gate_mine, opened(lists, (me ^ 1) * width, width)], axis=1)
    gates = gates.astype(F32)
    gates, gates_far = gates[:half_rows], gates[half_rows:]

    def forward(part, gate):
        return near(
            forward_kernel,
            (part, bias_row, gate, encoder_near, encoder_other, encoder_row, bias_other,
             decoder_near, decoder_other),
            (((half_rows, width), F32), ((half_rows, depth), BF16)),
        )

    preact_near, low = forward(rows, gates)
    preact_far, high = forward(after(low, rows_far), gates_far)
    every_row = jnp.concatenate([rows, after(high, rows_far)])
    rows_other = swap(every_row, 1)
    for bit in gathering[-2::-1]:
        low, high_received = lax.optimization_barrier(low + swap(low, bit | 1)), swap(high, bit | 1)
        high = lax.optimization_barrier(high + after(low, high_received))
    high_received = swap(low, gathering[-1] | 1)
    high, weights = lax.optimization_barrier((high, (encoder_weight, decoder_weight)))
    low_received = swap(high, gathering[-1] | 1)
    encoder_turned, decoder_turned = turn(*weights, encoder_other, decoder_other)

    errors, part = near(
        backward_kernel,
        (low, low_received, rows, gates, high, high_received, rows_far, gates_far, bias_row,
         encoder_turned, decoder_turned),
        (((2 * half_rows, depth), BF16), ((1, depth), F32)),
    )
    errors_other = swap(errors, 1)
    part = part + swap(part, 1)
    errors_other, part = lax.optimization_barrier((errors_other, part))

    rows_other, lists_other, threshold, _ = lax.optimization_barrier(
        (rows_other, lists_other, threshold, errors)
    )
    centered_other = center(rows_other)
    gate_rest = opened(lists_other, me * width, width)
    preact_rest = dot(centered_other, encoder_weight) + encoder_bias
    preact = jnp.concatenate([preact_near, preact_far, preact_rest])
    gate = jnp.concatenate([gate_mine, gate_rest])
    every_centered = jnp.concatenate([center(every_row), centered_other])
    codes = jnp.where(gate, preact, 0.0).astype(BF16)

    every_error = jnp.concatenate([errors, errors_other])

    def small_outputs():
        code_grad = dot_last(every_error, decoder_weight)
        distance = (preact - threshold) / EPSILON
        kernel = jnp.exp(-0.5 * distance * distance) / (EPSILON * math.sqrt(2.0 * math.pi))
        grad_threshold = jnp.sum(-threshold * code_grad * kernel - SPARSITY * kernel, axis=0)
        preact_grad = jnp.where(gate, code_grad, 0.0)
        return grad_threshold, jnp.sum(preact_grad, axis=0), preact_grad.astype(BF16)

    def decoder_output():
        return dot_rows(codes, every_error).astype(BF16)

    def encoder_output():
        return dot_rows(every_centered, small[2]).astype(BF16)

    part = part + swap(part, hops[0] | 1)
    small, part = lax.optimization_barrier((small_outputs(), part))
    part = part + swap(part, hops[1] | 1)
    grad_decoder, part = lax.optimization_barrier((decoder_output(), part))
    (error_sum,) = near(sum_kernel, (errors, errors_other), (((1, depth), F32),))
    for bit in hops[2:]:
        part = part + swap(part, bit | 1)
    grad_decoder_bias = (error_sum - part).reshape(depth)
    grad_encoder = encoder_output()
    grad_threshold, grad_encoder_bias, _ = small
    return (grad_encoder, grad_encoder_bias, grad_threshold, grad_decoder, grad_decoder_bias)


def solution(mesh):
    count = mesh.shape["latent"]

    def body(*args):
        return on_device(count, *args)

    placed = (
        P(("group", "latent"), None),
        P("group", None),
        P("group", "latent"),
        P(("group", "latent")),
        P(("group", "latent")),
        P(("group", "latent"), None),
        P("group"),
    )
    return jax.shard_map(
        body,
        mesh=mesh,
        in_specs=placed,
        out_specs=(
            P("group", "latent"),
            P(("group", "latent")),
            P(("group", "latent")),
            P(("group", "latent"), None),
            P("group"),
        ),
        check_vma=False,
    )
```
